256 devices in a mesh: dp: 4 (over x), section: 4 (over y), tensor: 16 (over z, core).
Axes of the slice: x: 4, y: 4, z: 8, core: 2. Of those that a mesh axis runs over, the one named last changes fastest.
Arguments:
- hidden_in: bfloat16 [2, 128, 8192], P(None, 'dp'), parts along dimension 1, may hold values from -3 to 3
- queries: bfloat16 [4, 2, 128, 8192], P('section', None, 'dp', 'tensor'), parts along dimension 2, may hold values from -16 to 16
- new_keys: bfloat16 [4, 2, 128, 2048], P('section', None, 'dp', 'tensor'), parts along dimension 2, may hold values from -6 to 6, as said below
- new_values: bfloat16 [4, 2, 128, 2048], P('section', None, 'dp', 'tensor'), parts along dimension 2, may hold values from -6 to 6, as said below
- cache_keys: bfloat16 [4, 128, 384, 2048], P('section', 'dp', None, 'tensor'), parts along dimension 1, may hold values from -12 to 12, as said below
- cache_values: bfloat16 [4, 128, 384, 2048], P('section', 'dp', None, 'tensor'), parts along dimension 1, may hold values from -6 to 6, as said below
- out_weight: bfloat16 [4, 8192, 8192], P('section', 'tensor'), may hold values from -0.75 to 0.75
- cache_lengths: int32 [128], P('dp'), parts along dimension 0, may hold values from 2 to 384, as said below
- positions: int32 [128], P('dp'), parts along dimension 0, may hold values from 2 to 767, as said below
Outputs:
- section_states: bfloat16 [4, 2, 128, 8192], P('section', None, 'dp'), parts along dimension 2
The draws below stay inside these ranges and needn't reach their ends.
There are 4 independent parts, one for each index of `dp`. The reference program is written for one: setup_inputs(seed, part) draws one part's arguments, and reference() takes and returns one part's arrays. A program takes and returns all parts, laid end to end along the dimension named above; an argument that names none is the same for every part. Nothing has to cross between parts.
Inputs may be any that keep to these rules, and one draw needn't show every extreme that they name: `cache_keys`: column blocks 2 t and 2 t + 1 of 128 entries are equal: two devices hold copies of one key-value head. `cache_values`: column blocks 2 t and 2 t + 1 of 128 entries are equal. `new_keys`: column blocks 2 t and 2 t + 1 of 128 entries are equal. `new_values`: column blocks 2 t and 2 t + 1 of 128 entries are equal. `cache_lengths`: some sequence fills all 384 slots. `positions`: each sequence's position is at least its cache length.
All inputs are finite; a program needn't handle non-finite values. Where the reference program divides by a largest or mean magnitude, that divisor is 1e-20 or more.
Results may differ from the reference program's by a relative error of at most 0.02.
Values may be sent and summed in bfloat16 or wider, within the bound.
No kernel may reach another device: no remote copies, remote signals or barrier semaphores. Data moves between devices by JAX's collectives and lax.ppermute only.
A program may use at most 128 MiB of HBM per device.

```python
import jax
import jax.numpy as jnp
from jax import lax

D = 8192
HEAD_DIM = 128
HEADS_DEV = 4
BLOCK = 128
STEPS = 2
ROWS = 32
CACHE = 384
HEADS = 64
N_SECTION = 4
N_TENSOR = 16


def paired(key, leading, bound):
    pair_count = N_TENSOR // 2
    single = jnp.clip(jax.random.normal(key, leading + (pair_count, 1, HEAD_DIM), jnp.float32), -bound, bound)
    both = jnp.broadcast_to(single, leading + (pair_count, 2, HEAD_DIM))
    return both.reshape(leading + (N_TENSOR, HEAD_DIM))


def base_rows(key):
    lengths = jax.random.randint(jax.random.fold_in(key, 11), (ROWS,), 2, CACHE + 1)
    chosen = jax.random.randint(jax.random.fold_in(key, 12), (), 0, ROWS)
    marked = jnp.arange(ROWS) == chosen
    lengths = jnp.where(marked, CACHE, lengths)
    offsets = jax.random.randint(jax.random.fold_in(key, 13), (ROWS,), 0, CACHE)
    offsets = jnp.where(marked, CACHE - 1, offsets)
    return (lengths.astype(jnp.int32), (lengths + offsets).astype(jnp.int32))


def draw_cache_lengths(key, part):
    lengths, starts = base_rows(key)
    return lengths


def draw_positions(key, part):
    lengths, starts = base_rows(key)
    return starts


def draw_new_keys(key, part):
    key = jax.random.fold_in(key, 5)
    values = paired(key, (N_SECTION, STEPS, ROWS), 6.0)
    return values.reshape(N_SECTION, STEPS, ROWS, N_TENSOR * HEAD_DIM).astype(jnp.bfloat16)


def draw_new_values(key, part):
    key = jax.random.fold_in(key, 6)
    values = paired(key, (N_SECTION, STEPS, ROWS), 6.0)
    return values.reshape(N_SECTION, STEPS, ROWS, N_TENSOR * HEAD_DIM).astype(jnp.bfloat16)


def draw_cache_values(key, part):
    key = jax.random.fold_in(key, 7)
    values = paired(key, (N_SECTION, ROWS, CACHE), 6.0)
    return values.reshape(N_SECTION, ROWS, CACHE, N_TENSOR * HEAD_DIM).astype(jnp.bfloat16)


def draw_cache_keys(key, part):
    key = jax.random.fold_in(key, 3)
    keys = paired(key, (N_SECTION, ROWS, CACHE), 6.0).reshape(N_SECTION, ROWS, CACHE, N_TENSOR * HEAD_DIM)
    return keys.astype(jnp.bfloat16)


def draw_queries(key, part):
    key = jax.random.fold_in(key, 4)
    values = jnp.clip(jax.random.normal(key, (N_SECTION, STEPS, ROWS, N_TENSOR, HEADS_DEV, HEAD_DIM), jnp.float32), -6.0, 6.0)
    return values.reshape(N_SECTION, STEPS, ROWS, N_TENSOR * HEADS_DEV * HEAD_DIM).astype(jnp.bfloat16)


def with_spikes(array, key, source, target, blocks, factor):
    owner, partner = [(jnp.arange(array.shape[position]) // (array.shape[position] // blocks)).reshape([-1 if axis == position else 1 for axis in range(array.ndim)]) for position in (source, target)]
    chosen = jax.random.permutation(key, blocks)[partner]
    strong = (owner == chosen) | (owner == (partner + blocks // 2) % blocks)
    return jnp.where(strong, factor * array, array)


def levels(key, shape, shards, smallest, largest):
    def one(axis_at, blocks):
        draws = jax.random.uniform(jax.random.fold_in(jax.random.fold_in(key, 6), axis_at), (blocks,), jnp.float32, smallest / len(shards), largest / len(shards))
        return jnp.repeat(jnp.exp(draws), shape[axis_at] // blocks).reshape((-1,) + (1,) * (len(shape) - axis_at - 1))

    level = one(*shards[0])
    for cut in shards[1:]:
        level = level * one(*cut)
    return level


def bell_draw(rng, shape, scale, limit, split=(), kind=jnp.bfloat16):
    values = scale * jax.random.normal(rng, shape, jnp.float32)
    if split:
        values = values * levels(rng, shape, split, -0.22, 0.18)
    return jnp.clip(values, -limit, limit).astype(kind)


def noise_with(key, shape, width, limit, pieces, heavy, held_as=jnp.bfloat16):
    drawn = width * jax.random.normal(key, shape, jnp.float32)
    if pieces:
        drawn = drawn * levels(key, shape, pieces, -0.22, 0.18)
    return jnp.clip(with_spikes(drawn, jax.random.fold_in(key, 3), *heavy), -limit, limit).astype(held_as)


def setup_inputs(seed: int = 0, part: int = 0) -> dict:
    splits = jax.random.split(jax.random.key(seed), 10)
    part_keys = jax.random.split(jax.random.fold_in(splits[9], part), 10)
    hidden_in = bell_draw(part_keys[0], (STEPS, ROWS, D), 0.5, 3.0)
    queries = draw_queries(jax.random.fold_in(jax.random.fold_in(splits[9], part), 71), part)
    new_keys = draw_new_keys(jax.random.fold_in(jax.random.fold_in(splits[9], part), 71), part)
    new_values = draw_new_values(jax.random.fold_in(jax.random.fold_in(splits[9], part), 71), part)
    cache_keys = draw_cache_keys(jax.random.fold_in(jax.random.fold_in(splits[9], part), 71), part)
    cache_values = draw_cache_values(jax.random.fold_in(jax.random.fold_in(splits[9], part), 71), part)
    out_weight = noise_with(splits[6], (N_SECTION, HEADS * HEAD_DIM, D), HEAD_DIM ** -0.5, 0.75, ((0, 4), (1, 16)), (1, 2, 16, 2.0))
    cache_lengths = draw_cache_lengths(jax.random.fold_in(jax.random.fold_in(splits[9], part), 71), part)
    positions = draw_positions(jax.random.fold_in(jax.random.fold_in(splits[9], part), 71), part)
    return {"hidden_in": hidden_in, "queries": queries, "new_keys": new_keys, "new_values": new_values, "cache_keys": cache_keys, "cache_values": cache_values, "out_weight": out_weight, "cache_lengths": cache_lengths, "positions": positions}


def rotate(values, where_at):
    half = values.shape[-1] // 2
    rates = 500000.0 ** (-jnp.arange(half, dtype=jnp.float32) * 2.0 / values.shape[-1])
    angles = where_at[..., None] * rates
    cosine = jnp.cos(angles)
    sine = jnp.sin(angles)
    first = values[..., :half]
    second = values[..., half:]
    return jnp.concatenate([first * cosine - second * sine, second * cosine + first * sine], axis=-1)


def rounded(values):
    return lax.optimization_barrier(values.astype(jnp.bfloat16)).astype(jnp.float32)


def encoded(values):
    blocks = values.reshape(values.shape[:-1] + (values.shape[-1] // BLOCK, BLOCK))
    block_scale = rounded(jnp.max(jnp.abs(blocks), axis=-1, keepdims=True) + 1e-6)
    code_words = rounded(blocks / block_scale)
    return (code_words * block_scale).reshape(values.shape)


def reference(hidden_in, queries, new_keys, new_values, cache_keys, cache_values, out_weight, cache_lengths, positions):
    group_size = HEADS_DEV
    kv_count = N_TENSOR
    visible = jnp.arange(CACHE, dtype=jnp.int32)[None, :] < cache_lengths[:, None]
    angle_rows = positions.astype(jnp.float32)[None, :] + jnp.arange(STEPS, dtype=jnp.float32)[:, None]
    causal = jnp.arange(STEPS, dtype=jnp.int32)[:, None] >= jnp.arange(STEPS, dtype=jnp.int32)[None, :]
    factor = HEAD_DIM ** -0.5
    current = hidden_in.astype(jnp.float32)
    states = []
    for section in range(N_SECTION):
        query_rot = rounded(rotate(queries[section].astype(jnp.float32).reshape(STEPS, ROWS, kv_count, group_size, HEAD_DIM), angle_rows[:, :, None, None]))
        key_rot = rounded(rotate(new_keys[section].astype(jnp.float32).reshape(STEPS, ROWS, kv_count, HEAD_DIM), angle_rows[:, :, None]))
        fresh_values = new_values[section].astype(jnp.float32).reshape(STEPS, ROWS, kv_count, HEAD_DIM)
        past_keys = cache_keys[section].astype(jnp.float32).reshape(ROWS, CACHE, kv_count, HEAD_DIM)
        past_values = cache_values[section].astype(jnp.float32).reshape(ROWS, CACHE, kv_count, HEAD_DIM)
        past_scores = jnp.einsum('srkgd,rlkd->srkgl', query_rot, past_keys) * factor
        past_scores = jnp.where(visible[None, :, None, None, :], past_scores, -jnp.inf)
        fresh_scores = jnp.einsum('srkgd,mrkd->srkgm', query_rot, key_rot) * factor
        fresh_scores = jnp.where(causal[:, None, None, None, :], fresh_scores, -jnp.inf)
        highest = jnp.maximum(past_scores.max(-1), fresh_scores.max(-1))[..., None]
        past_exp = jnp.exp(past_scores - highest)
        fresh_exp = jnp.exp(fresh_scores - highest)
        total = past_exp.sum(-1, keepdims=True) + fresh_exp.sum(-1, keepdims=True)
        past_weights = rounded(past_exp / total)
        fresh_weights = rounded(fresh_exp / total)
        attended = jnp.einsum('srkgl,rlkd->srkgd', past_weights, past_values) + jnp.einsum('srkgm,mrkd->srkgd', fresh_weights, fresh_values)
        attended = rounded(attended).reshape(STEPS * ROWS, kv_count, group_size * HEAD_DIM)
        projection = out_weight[section].astype(jnp.float32).reshape(kv_count, group_size * HEAD_DIM, D)
        partials = jnp.einsum('rtc,tcd->trd', attended, projection)
        summed = jnp.sum(encoded(partials), axis=0)
        update = encoded(summed).reshape(STEPS, ROWS, D)
        current = rounded(current + update)
        states.append(current.astype(jnp.bfloat16))
    return jnp.stack(states)
```

```python
import jax
import jax.numpy as jnp
import numpy as np
from jax import lax
from jax.experimental import pallas as pl
from jax.experimental.pallas import tpu as pltpu
from jax.sharding import Mesh
from jax.sharding import PartitionSpec as P

CHUNK = 8


def attend_project(
    core_ref,
    length_ref,
    position_ref,
    rate_ref,
    query_ref,
    new_key_ref,
    new_value_ref,
    key_ref,
    value_ref,
    weight_ref,
    send_ref,
    keep_ref,
    angle,
    rotated,
    fresh0,
    fresh1,
    value0,
    value1,
    attended,
    weight,
    weight_sem,
):
    step = pl.program_id(0)
    steps, rows, _ = new_key_ref.shape[1:]
    head = new_key_ref.shape[3]
    group = query_ref.shape[3] // head
    per_row = steps * group
    blocks, _, width = send_ref.shape
    factor = head**-0.5
    core = core_ref[0]

    def fetch(side, block):
        half = (1 - core) if side == 0 else core
        column = pl.multiple_of((half * blocks + block) * width, width)
        return pltpu.make_async_copy(
            weight_ref.at[0, :, pl.ds(column, width)],
            weight.at[side * blocks + block],
            weight_sem.at[side * blocks + block],
        )

    @pl.when(step == 0)
    def _():
        for side in range(2):
            for block in range(blocks):
                fetch(side, block).start()
        rate = rate_ref[0:1, :]
        for row in range(rows):
            angle[row : row + 1, :] = position_ref[row].astype(jnp.float32) * jnp.ones_like(rate)
        sign = jnp.where(lax.broadcasted_iota(jnp.int32, (1, head), 1) < head // 2, -1.0, 1.0)
        cosines, sines = [], []
        for s in range(steps):
            turn = (angle[...] + float(s)) * rate
            cosines.append(jnp.cos(turn))
            sines.append(jnp.sin(turn) * sign)

        def rot(v, s):
            v = v.astype(jnp.float32)
            out = v * cosines[s] + pltpu.roll(v, head // 2, 1) * sines[s]
            return out.astype(jnp.bfloat16).astype(jnp.float32)

        keys = [rot(new_key_ref[0, s], s) for s in range(steps)]
        fresh = (fresh0, fresh1)
        fresh_values = (value0, value1)
        for s in range(steps):
            for g in range(group):
                k = s * group + g
                q = rot(query_ref[0, s, :, g * head : (g + 1) * head], s)
                at = pl.ds(k, rows, stride=per_row)
                rotated[at, :] = q
                for m in range(steps):
                    if m <= s:
                        score = jnp.sum(q * keys[m], axis=-1, keepdims=True) * factor
                        fresh[m][at, :] = jnp.broadcast_to(score, (rows, head))
                    else:
                        fresh[m][at, :] = jnp.full((rows, head), -jnp.inf, jnp.float32)
                    fresh_values[m][at, :] = new_value_ref[0, m].astype(jnp.float32)

    length = key_ref.shape[2]
    lane = lax.broadcasted_iota(jnp.int32, (per_row, length), 1)
    base = pl.multiple_of(step * (CHUNK * per_row), CHUNK * per_row)
    here = pl.ds(base, CHUNK * per_row)
    q_all = rotated[here, :].astype(jnp.bfloat16)
    scores = []
    for i in range(CHUNK):
        q = q_all[i * per_row : (i + 1) * per_row]
        score = lax.dot_general(
            q, key_ref[0, i], (((1,), (1,)), ((), ())), preferred_element_type=jnp.float32
        )
        visible = lane < length_ref[step * CHUNK + i]
        scores.append(jnp.where(visible, score * factor, -jnp.inf))
    scores = jnp.concatenate(scores, axis=0)
    new0 = fresh0[here, :]
    new1 = fresh1[here, :]
    highest = jnp.maximum(
        jnp.max(scores, axis=-1, keepdims=True), jnp.maximum(new0, new1)[:, 0:1]
    )
    past = jnp.exp(scores - highest)
    new0 = jnp.exp(new0 - highest)
    new1 = jnp.exp(new1 - highest)
    total = jnp.sum(past, axis=-1, keepdims=True) + (new0 + new1)[:, 0:1]
    past = (past / total).astype(jnp.bfloat16)
    new0 = (new0 / total).astype(jnp.bfloat16).astype(jnp.float32)
    new1 = (new1 / total).astype(jnp.bfloat16).astype(jnp.float32)
    results = []
    for i in range(CHUNK):
        results.append(
            jnp.dot(
                past[i * per_row : (i + 1) * per_row],
                value_ref[0, i],
                preferred_element_type=jnp.float32,
            )
        )
    attended[here, :] = (
        jnp.concatenate(results, axis=0) + new0 * value0[here, :] + new1 * value1[here, :]
    )

    @pl.when(step == pl.num_programs(0) - 1)
    def _():
        per_step = []
        for s in range(steps):
            per_step.append(
                jnp.concatenate(
                    [attended[pl.ds(s * group + g, rows, stride=per_row), :] for g in range(group)],
                    axis=1,
                )
            )
        left = jnp.concatenate(per_step, axis=0).astype(jnp.bfloat16)
        for block in range(blocks):
            fetch(0, block).wait()
            send_ref[block] = jnp.dot(
                left, weight[block], preferred_element_type=jnp.float32
            ).astype(send_ref.dtype)
        for block in range(blocks):
            fetch(1, block).wait()
            keep_ref[block] = jnp.dot(
                left, weight[blocks + block], preferred_element_type=jnp.float32
            )


def sum_blocks(got_ref, out_ref):
    total = got_ref[0].astype(jnp.float32)
    for i in range(1, got_ref.shape[0]):
        total = total + got_ref[i].astype(jnp.float32)
    out_ref[...] = total.astype(out_ref.dtype)


def add_sections(place_ref, hidden_ref, *refs):
    out_ref = refs[-1]
    rows = out_ref.shape[1]
    current = hidden_ref[...].reshape(rows, out_ref.shape[2]).astype(jnp.float32)
    for update in refs[:-1]:
        current = (current + update[...].astype(jnp.float32)).astype(jnp.bfloat16)
        current = current.astype(jnp.float32)
    current = current.astype(out_ref.dtype)
    for i in range(out_ref.shape[0]):
        out_ref[i] = current


def assemble(core_ref, own_ref, other_ref, out_ref):
    core = core_ref[0]
    blocks, _, width = own_ref.shape
    _, steps, rows, _ = out_ref.shape
    for block in range(blocks):
        at = pl.ds(pl.multiple_of((core * blocks + block) * width, width), width)
        out_ref[0, :, :, at] = own_ref[block].reshape(steps, rows, width)
        at = pl.ds(pl.multiple_of(((1 - core) * blocks + block) * width, width), width)
        out_ref[0, :, :, at] = other_ref[block].reshape(steps, rows, width)


VMEM = pl.BlockSpec(memory_space=pltpu.VMEM)
SMEM = pl.BlockSpec(memory_space=pltpu.SMEM)
SWAP = [(0, 1), (1, 0)]


def per_device(
    hidden_in,
    queries,
    new_keys,
    new_values,
    cache_keys,
    cache_values,
    out_weight,
    cache_lengths,
    positions,
):
    cores = lax.axis_size("core")
    chips = lax.axis_size("z")
    sections = lax.axis_size("section")
    steps, rows, model = hidden_in.shape
    length, head = cache_keys.shape[2:]
    group = queries.shape[3] // head
    depth = group * head
    share = model // (cores * chips)
    flat = steps * rows
    pairs = rows * steps * group
    core = lax.axis_index("core").astype(jnp.int32).reshape(1)
    half = head // 2
    rates = np.float32(500000.0) ** (-np.arange(half, dtype=np.float32) * np.float32(2.0 / head))
    rates = np.broadcast_to(np.concatenate([rates, rates]).astype(np.float32), (8, head))

    whole = lambda *shape: pl.BlockSpec(shape, lambda i: (0,) * len(shape))
    send, keep = pl.pallas_call(
        attend_project,
        grid=(rows // CHUNK,),
        out_shape=(
            jax.ShapeDtypeStruct((chips, flat, share), jnp.bfloat16),
            jax.ShapeDtypeStruct((chips, flat, share), jnp.float32),
        ),
        in_specs=[
            SMEM,
            SMEM,
            SMEM,
            whole(8, head),
            whole(1, steps, rows, depth),
            whole(1, steps, rows, head),
            whole(1, steps, rows, head),
            pl.BlockSpec((1, CHUNK, length, head), lambda i: (0, i, 0, 0)),
            pl.BlockSpec((1, CHUNK, length, head), lambda i: (0, i, 0, 0)),
            pl.BlockSpec(memory_space=pl.ANY),
        ],
        out_specs=(whole(chips, flat, share), whole(chips, flat, share)),
        scratch_shapes=[
            pltpu.VMEM((rows, head), jnp.float32),
            pltpu.VMEM((pairs, head), jnp.float32),
            pltpu.VMEM((pairs, head), jnp.float32),
            pltpu.VMEM((pairs, head), jnp.float32),
            pltpu.VMEM((pairs, head), jnp.float32),
            pltpu.VMEM((pairs, head), jnp.float32),
            pltpu.VMEM((pairs, head), jnp.float32),
            pltpu.VMEM((cores * chips, depth, share), jnp.bfloat16),
            pltpu.SemaphoreType.DMA((cores * chips,)),
        ],
        compiler_params=pltpu.CompilerParams(vmem_limit_bytes=40 * 2**20),
        name="attend_project",
    )(
        core,
        cache_lengths,
        positions,
        jnp.asarray(rates),
        queries,
        new_keys,
        new_values,
        cache_keys,
        cache_values,
        out_weight,
    )
    got = lax.ppermute(send, "core", SWAP)
    paired = (keep + got.astype(jnp.float32)).astype(jnp.bfloat16)
    parts = lax.all_to_all(paired, "z", 0, 0, tiled=True)
    update = pl.pallas_call(
        sum_blocks,
        out_shape=jax.ShapeDtypeStruct((flat, share), jnp.bfloat16),
        in_specs=[VMEM],
        out_specs=VMEM,
        name="sum_blocks",
    )(parts)
    updates = [
        lax.ppermute(update, "section", [(i, i + by) for i in range(sections - by)])
        for by in range(sections - 1, 0, -1)
    ] + [update]
    place = (core[0] * chips + lax.axis_index("z").astype(jnp.int32)).reshape(1)
    part = lambda: pl.BlockSpec((flat, share), lambda i, at: (0, 0))
    state = pl.pallas_call(
        add_sections,
        grid_spec=pltpu.PrefetchScalarGridSpec(
            num_scalar_prefetch=1,
            grid=(1,),
            in_specs=[pl.BlockSpec((steps, rows, share), lambda i, at: (0, 0, at[0]))]
            + [part() for _ in updates],
            out_specs=pl.BlockSpec((chips, flat, share), lambda i, at: (0, 0, 0)),
        ),
        out_shape=jax.ShapeDtypeStruct((chips, flat, share), jnp.bfloat16),
        name="add_sections",
    )(place, hidden_in, *updates)
    own = lax.all_to_all(state, "z", 0, 0, tiled=True)
    other = lax.ppermute(own, "core", SWAP)
    return pl.pallas_call(
        assemble,
        out_shape=jax.ShapeDtypeStruct((1, steps, rows, model), jnp.bfloat16),
        in_specs=[SMEM, VMEM, VMEM],
        out_specs=VMEM,
        name="assemble",
    )(core, own, other)


def solution(mesh):
    sizes = dict(mesh.shape)
    split = Mesh(
        mesh.devices.reshape(sizes["dp"], sizes["section"], sizes["tensor"] // 2, 2),
        ("dp", "section", "z", "core"),
    )
    tensor = ("z", "core")
    placed = (
        P(None, "dp", None),
        P("section", None, "dp", tensor),
        P("section", None, "dp", tensor),
        P("section", None, "dp", tensor),
        P("section", "dp", None, tensor),
        P("section", "dp", None, tensor),
        P("section", tensor, None),
        P("dp"),
        P("dp"),
    )
    return jax.shard_map(
        per_device,
        mesh=split,
        in_specs=placed,
        out_specs=P("section", None, "dp", None),
        check_vma=False,
    )
```

```python
import jax
import jax.numpy as jnp
import numpy as np
from jax import lax
from jax.experimental import pallas as pl
from jax.experimental.pallas import tpu as pltpu
from jax.sharding import Mesh
from jax.sharding import PartitionSpec as P

MIB = 2**20


def attend(
    core_ref,
    length_hbm,
    position_hbm,
    rate_hbm,
    query_hbm,
    new_key_hbm,
    new_value_hbm,
    key_hbm,
    value_hbm,
    weight_hbm,
    left_ref,
    send_ref,
    length_ref,
    position_ref,
    rate_ref,
    query_ref,
    new_key_ref,
    new_value_ref,
    key_ref,
    value_ref,
    weight_ref,
    angle,
    rotated,
    fresh0,
    fresh1,
    value0,
    value1,
    attended,
    small_sem,
    cache_sem,
    weight_sem,
):
    steps, rows, head = new_key_ref.shape[1:]
    group = query_ref.shape[3] // head
    length = key_ref.shape[1]
    per_row = steps * group
    blocks, _, width = send_ref.shape
    factor = head**-0.5
    other = 1 - core_ref[0]
    small = [
        pltpu.make_async_copy(source, target, small_sem.at[i])
        for i, (source, target) in enumerate(
            (
                (position_hbm, position_ref),
                (rate_hbm, rate_ref),
                (query_hbm, query_ref),
                (new_key_hbm, new_key_ref),
                (new_value_hbm, new_value_ref),
                (length_hbm, length_ref),
            )
        )
    ]
    caches = [
        pltpu.make_async_copy(key_hbm.at[0], key_ref, cache_sem.at[0]),
        pltpu.make_async_copy(value_hbm.at[0], value_ref, cache_sem.at[1]),
    ]
    weights = []
    for block in range(blocks):
        column = pl.multiple_of((other * blocks + block) * width, width)
        weights.append(
            pltpu.make_async_copy(
                weight_hbm.at[0, :, pl.ds(column, width)], weight_ref.at[block], weight_sem.at[block]
            )
        )
    for copy in small + caches + weights:
        copy.start()
    for copy in small:
        copy.wait()

    rate = rate_ref[...]
    for row in range(rows):
        angle[row : row + 1, :] = position_ref[row].astype(jnp.float32) * jnp.ones_like(rate)
    sign = jnp.where(lax.broadcasted_iota(jnp.int32, (1, head), 1) < head // 2, -1.0, 1.0)
    turns = [(angle[...] + float(s)) * rate for s in range(steps)]
    cosines = [jnp.cos(turn) for turn in turns]
    sines = [jnp.sin(turn) * sign for turn in turns]

    def rot(v, s):
        v = v.astype(jnp.float32)
        out = v * cosines[s] + pltpu.roll(v, head // 2, 1) * sines[s]
        return out.astype(jnp.bfloat16).astype(jnp.float32)

    keys = [rot(new_key_ref[0, s], s) for s in range(steps)]
    fresh = (fresh0, fresh1)
    fresh_values = (value0, value1)
    for s in range(steps):
        for g in range(group):
            at = pl.ds(s * group + g, rows, stride=per_row)
            q = rot(query_ref[0, s, :, g * head : (g + 1) * head], s)
            rotated[at, :] = q
            for m in range(steps):
                if m <= s:
                    score = jnp.sum(q * keys[m], axis=-1, keepdims=True) * factor
                    fresh[m][at, :] = jnp.broadcast_to(score, (rows, head))
                else:
                    fresh[m][at, :] = jnp.full((rows, head), -jnp.inf, jnp.float32)
                fresh_values[m][at, :] = new_value_ref[0, m].astype(jnp.float32)

    lane = lax.broadcasted_iota(jnp.int32, (per_row, length), 1)
    q_all = rotated[...].astype(jnp.bfloat16)
    caches[0].wait()
    scores = []
    for row in range(rows):
        score = lax.dot_general(
            q_all[row * per_row : (row + 1) * per_row],
            key_ref[row],
            (((1,), (1,)), ((), ())),
            preferred_element_type=jnp.float32,
        )
        scores.append(jnp.where(lane < length_ref[row], score * factor, -jnp.inf))
    scores = jnp.concatenate(scores, axis=0)
    new0 = fresh0[...]
    new1 = fresh1[...]
    highest = jnp.maximum(
        jnp.max(scores, axis=-1, keepdims=True), jnp.maximum(new0, new1)[:, 0:1]
    )
    past = jnp.exp(scores - highest)
    new0 = jnp.exp(new0 - highest)
    new1 = jnp.exp(new1 - highest)
    total = jnp.sum(past, axis=-1, keepdims=True) + (new0 + new1)[:, 0:1]
    scale = 1.0 / total
    past = (past * scale).astype(jnp.bfloat16)
    new0 = (new0 * scale).astype(jnp.bfloat16).astype(jnp.float32)
    new1 = (new1 * scale).astype(jnp.bfloat16).astype(jnp.float32)
    caches[1].wait()
    results = [
        jnp.dot(
            past[row * per_row : (row + 1) * per_row],
            value_ref[row],
            preferred_element_type=jnp.float32,
        )
        for row in range(rows)
    ]
    attended[...] = jnp.concatenate(results, axis=0) + new0 * value0[...] + new1 * value1[...]
    left = jnp.concatenate(
        [
            jnp.concatenate(
                [attended[pl.ds(s * group + g, rows, stride=per_row), :] for g in range(group)],
                axis=1,
            )
            for s in range(steps)
        ],
        axis=0,
    ).astype(jnp.bfloat16)
    left_ref[...] = left
    for block in range(blocks):
        weights[block].wait()
        send_ref[block] = jnp.dot(
            left, weight_ref[block], preferred_element_type=jnp.float32
        ).astype(send_ref.dtype)


def project(core_ref, left_ref, weight_hbm, keep_ref, weight_ref, weight_sem):
    blocks, _, width = keep_ref.shape
    copies = []
    for block in range(blocks):
        column = pl.multiple_of((core_ref[0] * blocks + block) * width, width)
        copies.append(
            pltpu.make_async_copy(
                weight_hbm.at[0, :, pl.ds(column, width)], weight_ref.at[block], weight_sem.at[block]
            )
        )
    for copy in copies:
        copy.start()
    for block in range(blocks):
        copies[block].wait()
        keep_ref[block] = jnp.dot(
            left_ref[...], weight_ref[block], preferred_element_type=jnp.float32
        )


def assemble(core_ref, own_ref, other_ref, out_ref, sem):
    blocks, _, width = own_ref.shape
    _, steps, rows, _ = out_ref.shape
    copies = []
    for side, ref in enumerate((own_ref, other_ref)):
        half = core_ref[0] if side == 0 else 1 - core_ref[0]
        for s in range(steps):
            for block in range(blocks):
                at = pl.ds(pl.multiple_of((half * blocks + block) * width, width), width)
                copies.append(
                    pltpu.make_async_copy(
                        ref.at[block, s * rows : (s + 1) * rows],
                        out_ref.at[0, s, :, at],
                        sem.at[side, s, block],
                    )
                )
    for copy in copies:
        copy.start()
    for copy in copies:
        copy.wait()


VMEM = pl.BlockSpec(memory_space=pltpu.VMEM)
SMEM = pl.BlockSpec(memory_space=pltpu.SMEM)
HBM = pl.BlockSpec(memory_space=pltpu.HBM)
ANY = pl.BlockSpec(memory_space=pl.ANY)
SWAP = [(0, 1), (1, 0)]


def per_device(
    hidden_in,
    queries,
    new_keys,
    new_values,
    cache_keys,
    cache_values,
    out_weight,
    cache_lengths,
    positions,
):
    cores = lax.axis_size("core")
    chips = lax.axis_size("z")
    sections = lax.axis_size("section")
    steps, rows, model = hidden_in.shape
    length, head = cache_keys.shape[2:]
    group = queries.shape[3] // head
    depth = group * head
    share = model // (cores * chips)
    flat = steps * rows
    pairs = rows * steps * group
    core = lax.axis_index("core").astype(jnp.int32).reshape(1)
    half = head // 2
    rates = np.float32(500000.0) ** (-np.arange(half, dtype=np.float32) * np.float32(2.0 / head))
    rates = np.concatenate([rates, rates]).astype(np.float32)[None]
    left, send = pl.pallas_call(
        attend,
        out_shape=(
            jax.ShapeDtypeStruct((flat, depth), jnp.bfloat16),
            jax.ShapeDtypeStruct((chips, flat, share), jnp.bfloat16),
        ),
        in_specs=[SMEM] + [HBM] * 9,
        out_specs=(VMEM, VMEM),
        scratch_shapes=[
            pltpu.SMEM((rows,), jnp.int32),
            pltpu.SMEM((rows,), jnp.int32),
            pltpu.VMEM((1, head), jnp.float32),
            pltpu.VMEM(queries.shape, jnp.bfloat16),
            pltpu.VMEM(new_keys.shape, jnp.bfloat16),
            pltpu.VMEM(new_values.shape, jnp.bfloat16),
            pltpu.VMEM((rows, length, head), jnp.bfloat16),
            pltpu.VMEM((rows, length, head), jnp.bfloat16),
            pltpu.VMEM((chips, depth, share), jnp.bfloat16),
            pltpu.VMEM((rows, head), jnp.float32),
        ]
        + [pltpu.VMEM((pairs, head), jnp.float32)] * 6
        + [
            pltpu.SemaphoreType.DMA((6,)),
            pltpu.SemaphoreType.DMA((2,)),
            pltpu.SemaphoreType.DMA((chips,)),
        ],
        compiler_params=pltpu.CompilerParams(vmem_limit_bytes=59 * MIB),
        name="attend",
    )(
        core,
        cache_lengths,
        positions,
        jnp.asarray(rates),
        queries,
        new_keys,
        new_values,
        cache_keys,
        cache_values,
        out_weight,
    )
    got = lax.ppermute(send, "core", SWAP)
    keep = pl.pallas_call(
        project,
        out_shape=jax.ShapeDtypeStruct((chips, flat, share), jnp.float32),
        in_specs=[SMEM, VMEM, HBM],
        out_specs=VMEM,
        scratch_shapes=[
            pltpu.VMEM((chips, depth, share), jnp.bfloat16),
            pltpu.SemaphoreType.DMA((chips,)),
        ],
        cost_estimate=pl.CostEstimate(
            flops=flat * depth * model, bytes_accessed=depth * model, transcendentals=0
        ),
        compiler_params=pltpu.CompilerParams(vmem_limit_bytes=56 * MIB),
        name="project",
    )(core, left, out_weight)
    paired = (keep + got.astype(jnp.float32)).astype(jnp.bfloat16)
    parts = lax.all_to_all(paired, "z", 0, 0, tiled=True)
    update = jnp.sum(parts.astype(jnp.float32), axis=0).astype(jnp.bfloat16)
    updates = [
        lax.ppermute(update, "section", [(i, i + by) for i in range(sections - by)])
        for by in range(sections - 1, 0, -1)
    ] + [update]
    place = (core[0] * chips + lax.axis_index("z").astype(jnp.int32)) * share
    current = lax.dynamic_slice(hidden_in, (0, 0, place), (steps, rows, share)).reshape(flat, share)
    for term in updates:
        current = (current.astype(jnp.float32) + term.astype(jnp.float32)).astype(jnp.bfloat16)
    state = jnp.broadcast_to(current, (chips, flat, share))
    own = lax.all_to_all(state, "z", 0, 0, tiled=True)
    other = lax.ppermute(own, "core", SWAP)
    return pl.pallas_call(
        assemble,
        out_shape=jax.ShapeDtypeStruct((1, steps, rows, model), jnp.bfloat16),
        in_specs=[SMEM, ANY, ANY],
        out_specs=HBM,
        scratch_shapes=[pltpu.SemaphoreType.DMA((2, steps, chips))],
        compiler_params=pltpu.CompilerParams(vmem_limit_bytes=MIB),
        name="assemble",
    )(core, own, other)


def solution(mesh):
    sizes = dict(mesh.shape)
    split = Mesh(
        mesh.devices.reshape(sizes["dp"], sizes["section"], sizes["tensor"] // 2, 2),
        ("dp", "section", "z", "core"),
    )
    tensor = ("z", "core")
    placed = (
        P(None, "dp", None),
        P("section", None, "dp", tensor),
        P("section", None, "dp", tensor),
        P("section", None, "dp", tensor),
        P("section", "dp", None, tensor),
        P("section", "dp", None, tensor),
        P("section", tensor, None),
        P("dp"),
        P("dp"),
    )
    return jax.shard_map(
        per_device,
        mesh=split,
        in_specs=placed,
        out_specs=P("section", None, "dp", None),
        check_vma=False,
    )
```

```python
import jax
import jax.numpy as jnp
import numpy as np
from jax import lax
from jax.experimental import pallas as pl
from jax.experimental.pallas import tpu as pltpu
from jax.sharding import Mesh
from jax.sharding import PartitionSpec as P

KIB = 1024
OFFSETS = (-2, 1, 4, -1, 2, -3, 0, 3)
TO_UP, TO_DOWN, STAY = slice(0, 3), slice(3, 5), slice(5, 8)
GROUP = 4


def attend(
    core_ref,
    chip_ref,
    length_hbm,
    position_hbm,
    rate_hbm,
    query_hbm,
    new_key_hbm,
    new_value_hbm,
    key_hbm,
    value_hbm,
    weight_hbm,
    hidden_hbm,
    send_ref,
    keep_ref,
    near_ref,
    length_ref,
    position_ref,
    rate_ref,
    query_ref,
    new_key_ref,
    new_value_ref,
    key_ref,
    value_ref,
    weight_ref,
    rotated,
    fresh0,
    fresh1,
    value0,
    value1,
    lengths,
    turns,
    attended,
    small_sem,
    hidden_sem,
    cache_sem,
    weight_sem,
):
    rows, length, head = key_ref.shape
    flat, width = near_ref.shape
    steps = flat // rows
    depth = weight_ref.shape[1]
    group = depth // head
    per_row = steps * group
    chips = send_ref.shape[0]
    factor = head**-0.5
    core = core_ref[0]
    chip = chip_ref[0]

    def columns(half, offset):
        block = half * chips + lax.rem(chip + (offset + chips), chips)
        return pl.ds(pl.multiple_of(block * width, width), width)

    small = [
        pltpu.make_async_copy(source, target, small_sem.at[i])
        for i, (source, target) in enumerate(
            (
                (position_hbm, position_ref),
                (rate_hbm, rate_ref),
                (length_hbm, length_ref),
                (new_key_hbm, new_key_ref),
                (query_hbm, query_ref),
                (new_value_hbm, new_value_ref),
            )
        )
    ]
    caches = [
        pltpu.make_async_copy(key_hbm.at[0], key_ref, cache_sem.at[0]),
        pltpu.make_async_copy(value_hbm.at[0], value_ref, cache_sem.at[1]),
    ]
    weights = []
    for half in (1 - core, core):
        for offset in OFFSETS:
            slot = len(weights)
            weights.append(
                pltpu.make_async_copy(
                    weight_hbm.at[0, :, columns(half, offset)],
                    weight_ref.at[slot],
                    weight_sem.at[slot],
                )
            )
    hidden = [
        pltpu.make_async_copy(
            hidden_hbm.at[s, :, columns(core, 0)],
            near_ref.at[s * rows : (s + 1) * rows],
            hidden_sem.at[s],
        )
        for s in range(steps)
    ]
    for copy in small + caches:
        copy.start()

    for copy in small:
        copy.wait()
    for row in range(rows):
        for s in range(steps):
            at = s * rows + row
            when = (position_ref[row] + s).astype(jnp.float32)
            turns[at : at + 1, :] = jnp.full((1, head), when, jnp.float32)
        limit = length_ref[row].astype(jnp.float32)
        lengths[row * per_row : (row + 1) * per_row, :] = jnp.full((per_row, head), limit, jnp.float32)
    sign = jnp.where(lax.broadcasted_iota(jnp.int32, (1, head), 1) < head // 2, -1.0, 1.0)
    turn = turns[...] * rate_ref[...]
    cosine = jnp.cos(turn)
    sine = jnp.sin(turn) * sign

    def rot(v):
        v = v.astype(jnp.float32).reshape(flat, head)
        out = v * cosine + pltpu.roll(v, head // 2, 1) * sine
        return out.astype(jnp.bfloat16).astype(jnp.float32)

    keys = rot(new_key_ref[0])
    fresh = (fresh0, fresh1)
    fresh_values = (value0, value1)
    for g in range(group):
        q = rot(query_ref[0, :, :, g * head : (g + 1) * head])
        for s in range(steps):
            at = pl.ds(s * group + g, rows, stride=per_row)
            mine = q[s * rows : (s + 1) * rows]
            rotated[at, :] = mine
            for m in range(steps):
                if m <= s:
                    score = jnp.sum(mine * keys[m * rows : (m + 1) * rows], axis=-1, keepdims=True)
                    fresh[m][at, :] = jnp.broadcast_to(score * factor, (rows, head))
                else:
                    fresh[m][at, :] = jnp.full((rows, head), -jnp.inf, jnp.float32)
                fresh_values[m][at, :] = new_value_ref[0, m].astype(jnp.float32)

    q_all = rotated[...].astype(jnp.bfloat16)
    caches[0].wait()
    for copy in weights[:chips]:
        copy.start()
    scores = jnp.concatenate(
        [
            lax.dot_general(
                q_all[row * per_row : (row + 1) * per_row],
                key_ref[row],
                (((1,), (1,)), ((), ())),
                preferred_element_type=jnp.float32,
            )
            for row in range(rows)
        ],
        axis=0,
    )
    lane = lax.broadcasted_iota(jnp.int32, (1, length), 1).astype(jnp.float32)
    limit = jnp.concatenate([lengths[...]] * (length // head), axis=1)
    scores = jnp.where(lane < limit, scores * factor, -jnp.inf)
    new0 = fresh0[...]
    new1 = fresh1[...]
    highest = jnp.maximum(
        jnp.max(scores, axis=-1, keepdims=True), jnp.maximum(new0, new1)[:, 0:1]
    )
    past = jnp.exp(scores - highest)
    new0 = jnp.exp(new0 - highest)
    new1 = jnp.exp(new1 - highest)
    total = jnp.sum(past, axis=-1, keepdims=True) + (new0 + new1)[:, 0:1]
    scale = 1.0 / total
    past = (past * scale).astype(jnp.bfloat16)
    new0 = (new0 * scale).astype(jnp.bfloat16).astype(jnp.float32)
    new1 = (new1 * scale).astype(jnp.bfloat16).astype(jnp.float32)
    caches[1].wait()
    for copy in weights[chips:] + hidden:
        copy.start()
    results = jnp.concatenate(
        [
            jnp.dot(
                past[row * per_row : (row + 1) * per_row],
                value_ref[row],
                preferred_element_type=jnp.float32,
            )
            for row in range(rows)
        ],
        axis=0,
    )
    attended[...] = results + new0 * value0[...] + new1 * value1[...]
    left = jnp.concatenate(
        [
            jnp.concatenate(
                [attended[pl.ds(s * group + g, rows, stride=per_row), :] for g in range(group)],
                axis=1,
            )
            for s in range(steps)
        ],
        axis=0,
    ).astype(jnp.bfloat16)
    for first in range(0, len(weights), GROUP):
        for slot in range(first, first + GROUP):
            weights[slot].wait()
        for slot in range(first, first + GROUP):
            partial = jnp.dot(left, weight_ref[slot], preferred_element_type=jnp.float32)
            target = send_ref if slot < chips else keep_ref
            target[slot % chips] = partial.astype(target.dtype)
    for copy in hidden:
        copy.wait()


PIECES = (
    (False, (3,)),
    (False, (0,)),
    (False, (-3,)),
    (False, (2, -1, -4)),
    (False, (1, -2)),
    (True, (3, 0, -3)),
    (True, (2, -1, -4)),
    (True, (1, -2)),
)


def assemble(core_ref, chip_ref, *refs):
    parts, out_ref, sem = refs[:-2], refs[-2], refs[-1]
    core, chip = core_ref[0], chip_ref[0]
    model = out_ref.shape[1]
    copies = []
    for ref, (swapped, offsets) in zip(parts, PIECES):
        half = 1 - core if swapped else core
        width = ref.shape[-1]
        chips = model // width // 2
        for i, offset in enumerate(offsets):
            block = half * chips + lax.rem(chip + (offset + chips), chips)
            at = pl.ds(pl.multiple_of(block * width, width), width)
            copies.append(
                pltpu.make_async_copy(ref.at[i], out_ref.at[:, at], sem.at[len(copies)])
            )
    for copy in copies:
        copy.start()
    for copy in copies:
        copy.wait()


VMEM = pl.BlockSpec(memory_space=pltpu.VMEM)
SMEM = pl.BlockSpec(memory_space=pltpu.SMEM)
HBM = pl.BlockSpec(memory_space=pltpu.HBM)
ANY = pl.BlockSpec(memory_space=pl.ANY)
SWAP = [(0, 1), (1, 0)]


def widen(array):
    return array.astype(jnp.float32)


def narrow(array):
    return array.astype(jnp.bfloat16)


def per_device(
    hidden_in,
    queries,
    new_keys,
    new_values,
    cache_keys,
    cache_values,
    out_weight,
    cache_lengths,
    positions,
):
    cores = lax.axis_size("core")
    chips = lax.axis_size("z")
    sections = lax.axis_size("section")
    steps, rows, model = hidden_in.shape
    length, head = cache_keys.shape[2:]
    depth = queries.shape[3]
    share = model // (cores * chips)
    flat = steps * rows
    pairs = flat * depth // head
    half = head // 2
    rates = np.float32(500000.0) ** (-np.arange(half, dtype=np.float32) * np.float32(2.0 / head))
    rates = np.concatenate([rates, rates]).astype(np.float32)[None]
    core = lax.axis_index("core").astype(jnp.int32).reshape(1)
    chip = lax.axis_index("z").astype(jnp.int32).reshape(1)

    def shift(array, by):
        return lax.ppermute(array, "z", [(i, (i + by) % chips) for i in range(chips)])

    send, keep, current = pl.pallas_call(
        attend,
        out_shape=(
            jax.ShapeDtypeStruct((chips, flat, share), jnp.bfloat16),
            jax.ShapeDtypeStruct((chips, flat, share), jnp.float32),
            jax.ShapeDtypeStruct((flat, share), jnp.bfloat16),
        ),
        in_specs=[SMEM, SMEM] + [HBM] * 10,
        out_specs=(VMEM, VMEM, VMEM),
        scratch_shapes=[
            pltpu.SMEM((rows,), jnp.int32),
            pltpu.SMEM((rows,), jnp.int32),
            pltpu.VMEM((1, head), jnp.float32),
            pltpu.VMEM(queries.shape, jnp.bfloat16),
            pltpu.VMEM(new_keys.shape, jnp.bfloat16),
            pltpu.VMEM(new_values.shape, jnp.bfloat16),
            pltpu.VMEM((rows, length, head), jnp.bfloat16),
            pltpu.VMEM((rows, length, head), jnp.bfloat16),
            pltpu.VMEM((cores * chips, depth, share), jnp.bfloat16),
        ]
        + [pltpu.VMEM((pairs, head), jnp.float32)] * 6
        + [
            pltpu.VMEM((flat, head), jnp.float32),
            pltpu.VMEM((pairs, head), jnp.float32),
            pltpu.SemaphoreType.DMA((6,)),
            pltpu.SemaphoreType.DMA((steps,)),
            pltpu.SemaphoreType.DMA((2,)),
            pltpu.SemaphoreType.DMA((cores * chips,)),
        ],
        compiler_params=pltpu.CompilerParams(vmem_limit_bytes=58368 * KIB),
        name="attend",
    )(
        core,
        chip,
        cache_lengths,
        positions,
        jnp.asarray(rates),
        queries,
        new_keys,
        new_values,
        cache_keys,
        cache_values,
        out_weight,
        hidden_in,
    )

    got = lax.ppermute(send, "core", SWAP)
    paired = lambda part: keep[part] + widen(got[part])
    up = shift(narrow(paired(TO_UP)), 1)
    down = shift(narrow(paired(TO_DOWN)), -1)
    stay = paired(STAY)
    above = shift(narrow(stay[2] + widen(up[2]) + widen(down[1])), 3)
    below = shift(narrow(stay[0] + widen(up[0])), -3)
    update = narrow(stay[1] + widen(up[1]) + widen(down[0]) + widen(above) + widen(below))
    updates = [
        lax.ppermute(update, "section", [(i, i + by) for i in range(sections - by)])
        for by in (1,2,3)
    ]
    updates = [updates[(1,2,3).index(by)] for by in range(sections - 1, 0, -1)] + [update]
    for term in updates:
        current = narrow(widen(current) + widen(term))
    mine = current[None]
    near = [shift(mine, -3), mine, shift(mine, 3)]
    up = shift(jnp.concatenate(near), 1)
    down = shift(jnp.concatenate(near[1:]), -1)
    pieces = near + [up, down]
    pieces = pieces + [
        lax.ppermute(piece, "core", SWAP)
        for piece in (jnp.concatenate(near), up, down)
    ]
    states = pl.pallas_call(
        assemble,
        out_shape=jax.ShapeDtypeStruct((flat, model), jnp.bfloat16),
        in_specs=[SMEM, SMEM] + [ANY] * len(pieces),
        out_specs=HBM,
        scratch_shapes=[pltpu.SemaphoreType.DMA((cores * chips,))],
        compiler_params=pltpu.CompilerParams(vmem_limit_bytes=1024 * KIB),
        name="assemble",
    )(core, chip, *pieces)
    return states.reshape(1, steps, rows, model)


def solution(mesh):
    sizes = dict(mesh.shape)
    split = Mesh(
        mesh.devices.reshape(sizes["dp"], sizes["section"], sizes["tensor"] // 2, 2),
        ("dp", "section", "z", "core"),
    )
    tensor = ("z", "core")
    placed = (
        P(None, "dp", None),
        P("section", None, "dp", tensor),
        P("section", None, "dp", tensor),
        P("section", None, "dp", tensor),
        P("section", "dp", None, tensor),
        P("section", "dp", None, tensor),
        P("section", tensor, None),
        P("dp"),
        P("dp"),
    )
    return jax.shard_map(
        per_device,
        mesh=split,
        in_specs=placed,
        out_specs=P("section", None, "dp", None),
        check_vma=False,
    )
```

```python
import jax
import jax.numpy as jnp
import numpy as np
from jax import lax
from jax.experimental import pallas as pl
from jax.experimental.pallas import tpu as pltpu
from jax.sharding import Mesh
from jax.sharding import PartitionSpec as P

KIB = 1024
OFFSETS = (-2, 1, 4, -1, 2, -3, 0, 3)
TO_UP, TO_DOWN, STAY = slice(0, 3), slice(3, 5), slice(5, 8)
GROUP = 4


def attend(
    core_ref,
    chip_ref,
    length_hbm,
    position_hbm,
    rate_hbm,
    query_hbm,
    new_key_hbm,
    new_value_hbm,
    key_hbm,
    value_hbm,
    weight_hbm,
    hidden_hbm,
    send_ref,
    keep_ref,
    near_ref,
    length_ref,
    position_ref,
    rate_ref,
    query_ref,
    new_key_ref,
    new_value_ref,
    key_ref,
    value_ref,
    weight_ref,
    rotated,
    fresh0,
    fresh1,
    value0,
    value1,
    lengths,
    turns,
    attended,
    small_sem,
    hidden_sem,
    cache_sem,
    weight_sem,
):
    rows, length, head = key_ref.shape
    flat, width = near_ref.shape
    steps = flat // rows
    depth = weight_ref.shape[1]
    group = depth // head
    per_row = steps * group
    chips = send_ref.shape[0]
    factor = head**-0.5
    core = core_ref[0]
    chip = chip_ref[0]

    def columns(half, offset):
        block = half * chips + lax.rem(chip + (offset + chips), chips)
        return pl.ds(pl.multiple_of(block * width, width), width)

    small = [
        pltpu.make_async_copy(source, target, small_sem.at[i])
        for i, (source, target) in enumerate(
            (
                (position_hbm, position_ref),
                (rate_hbm, rate_ref),
                (length_hbm, length_ref),
                (new_key_hbm, new_key_ref),
                (query_hbm, query_ref),
                (new_value_hbm, new_value_ref),
            )
        )
    ]
    caches = [
        pltpu.make_async_copy(key_hbm.at[0], key_ref, cache_sem.at[0]),
        pltpu.make_async_copy(value_hbm.at[0], value_ref, cache_sem.at[1]),
    ]
    weights = []
    for half in (1 - core, core):
        for offset in OFFSETS:
            slot = len(weights)
            weights.append(
                pltpu.make_async_copy(
                    weight_hbm.at[0, :, columns(half, offset)],
                    weight_ref.at[slot],
                    weight_sem.at[slot],
                )
            )
    hidden = [
        pltpu.make_async_copy(
            hidden_hbm.at[s, :, columns(core, 0)],
            near_ref.at[s * rows : (s + 1) * rows],
            hidden_sem.at[s],
        )
        for s in range(steps)
    ]
    for copy in small + caches:
        copy.start()

    for copy in small:
        copy.wait()
    for row in range(rows):
        for s in range(steps):
            at = s * rows + row
            when = (position_ref[row] + s).astype(jnp.float32)
            turns[at : at + 1, :] = jnp.full((1, head), when, jnp.float32)
        limit = length_ref[row].astype(jnp.float32)
        lengths[row * per_row : (row + 1) * per_row, :] = jnp.full((per_row, head), limit, jnp.float32)
    sign = jnp.where(lax.broadcasted_iota(jnp.int32, (1, head), 1) < head // 2, -1.0, 1.0)
    turn = turns[...] * rate_ref[...]
    cosine = jnp.cos(turn)
    sine = jnp.sin(turn) * sign

    def rot(v):
        v = v.astype(jnp.float32).reshape(flat, head)
        out = v * cosine + pltpu.roll(v, head // 2, 1) * sine
        return out.astype(jnp.bfloat16).astype(jnp.float32)

    keys = rot(new_key_ref[0])
    fresh = (fresh0, fresh1)
    fresh_values = (value0, value1)
    for g in range(group):
        q = rot(query_ref[0, :, :, g * head : (g + 1) * head])
        for s in range(steps):
            at = pl.ds(s * group + g, rows, stride=per_row)
            mine = q[s * rows : (s + 1) * rows]
            rotated[at, :] = mine
            for m in range(steps):
                if m <= s:
                    score = jnp.sum(mine * keys[m * rows : (m + 1) * rows], axis=-1, keepdims=True)
                    fresh[m][at, :] = jnp.broadcast_to(score * factor, (rows, head))
                else:
                    fresh[m][at, :] = jnp.full((rows, head), -jnp.inf, jnp.float32)
                fresh_values[m][at, :] = new_value_ref[0, m].astype(jnp.float32)

    q_all = rotated[...].astype(jnp.bfloat16)
    caches[0].wait()
    for copy in weights[:chips]:
        copy.start()
    scores = jnp.concatenate(
        [
            lax.dot_general(
                q_all[row * per_row : (row + 1) * per_row],
                key_ref[row],
                (((1,), (1,)), ((), ())),
                preferred_element_type=jnp.float32,
            )
            for row in range(rows)
        ],
        axis=0,
    )
    lane = lax.broadcasted_iota(jnp.int32, (1, length), 1).astype(jnp.float32)
    limit = jnp.concatenate([lengths[...]] * (length // head), axis=1)
    scores = jnp.where(lane < limit, scores * factor, -jnp.inf)
    new0 = fresh0[...]
    new1 = fresh1[...]
    highest = jnp.maximum(
        jnp.max(scores, axis=-1, keepdims=True), jnp.maximum(new0, new1)[:, 0:1]
    )
    past = jnp.exp(scores - highest)
    new0 = jnp.exp(new0 - highest)
    new1 = jnp.exp(new1 - highest)
    total = jnp.sum(past, axis=-1, keepdims=True) + (new0 + new1)[:, 0:1]
    scale = 1.0 / total
    past = (past * scale).astype(jnp.bfloat16)
    new0 = (new0 * scale).astype(jnp.bfloat16).astype(jnp.float32)
    new1 = (new1 * scale).astype(jnp.bfloat16).astype(jnp.float32)
    caches[1].wait()
    for copy in weights[chips:] + hidden:
        copy.start()
    results = jnp.concatenate(
        [
            jnp.dot(
                past[row * per_row : (row + 1) * per_row],
                value_ref[row],
                preferred_element_type=jnp.float32,
            )
            for row in range(rows)
        ],
        axis=0,
    )
    attended[...] = results + new0 * value0[...] + new1 * value1[...]
    left = jnp.concatenate(
        [
            jnp.concatenate(
                [attended[pl.ds(s * group + g, rows, stride=per_row), :] for g in range(group)],
                axis=1,
            )
            for s in range(steps)
        ],
        axis=0,
    ).astype(jnp.bfloat16)
    for first in range(0, len(weights), GROUP):
        for slot in range(first, first + GROUP):
            weights[slot].wait()
        for slot in range(first, first + GROUP):
            partial = jnp.dot(left, weight_ref[slot], preferred_element_type=jnp.float32)
            target = send_ref if slot < chips else keep_ref
            target[slot % chips] = partial.astype(target.dtype)
    for copy in hidden:
        copy.wait()


PIECES = (
    (False, (3,)),
    (False, (0,)),
    (False, (-3,)),
    (False, (2, -1, -4)),
    (False, (1, -2)),
    (True, (3, 0, -3)),
    (True, (2, -1, -4)),
    (True, (1, -2)),
)


def assemble(core_ref, chip_ref, *refs):
    parts, out_ref, sem = refs[:-2], refs[-2], refs[-1]
    core, chip = core_ref[0], chip_ref[0]
    model = out_ref.shape[1]
    copies = []
    for ref, (swapped, offsets) in zip(parts, PIECES):
        half = 1 - core if swapped else core
        width = ref.shape[-1]
        chips = model // width // 2
        for i, offset in enumerate(offsets):
            block = half * chips + lax.rem(chip + (offset + chips), chips)
            at = pl.ds(pl.multiple_of(block * width, width), width)
            copies.append(
                pltpu.make_async_copy(ref.at[i], out_ref.at[:, at], sem.at[len(copies)])
            )
    for copy in copies:
        copy.start()
    for copy in copies:
        copy.wait()


VMEM = pl.BlockSpec(memory_space=pltpu.VMEM)
SMEM = pl.BlockSpec(memory_space=pltpu.SMEM)
HBM = pl.BlockSpec(memory_space=pltpu.HBM)
ANY = pl.BlockSpec(memory_space=pl.ANY)
SWAP = [(0, 1), (1, 0)]


def widen(array):
    return array.astype(jnp.float32)


def narrow(array):
    return array.astype(jnp.bfloat16)


def per_device(
    hidden_in,
    queries,
    new_keys,
    new_values,
    cache_keys,
    cache_values,
    out_weight,
    cache_lengths,
    positions,
):
    cores = lax.axis_size("core")
    chips = lax.axis_size("z")
    sections = lax.axis_size("section")
    steps, rows, model = hidden_in.shape
    length, head = cache_keys.shape[2:]
    depth = queries.shape[3]
    share = model // (cores * chips)
    flat = steps * rows
    pairs = flat * depth // head
    half = head // 2
    rates = np.float32(500000.0) ** (-np.arange(half, dtype=np.float32) * np.float32(2.0 / head))
    rates = np.concatenate([rates, rates]).astype(np.float32)[None]
    core = lax.axis_index("core").astype(jnp.int32).reshape(1)
    chip = lax.axis_index("z").astype(jnp.int32).reshape(1)

    def shift(array, by):
        return lax.ppermute(array, "z", [(i, (i + by) % chips) for i in range(chips)])

    send, keep, current = pl.pallas_call(
        attend,
        out_shape=(
            jax.ShapeDtypeStruct((chips, flat, share), jnp.bfloat16),
            jax.ShapeDtypeStruct((chips, flat, share), jnp.float32),
            jax.ShapeDtypeStruct((flat, share), jnp.bfloat16),
        ),
        in_specs=[SMEM, SMEM] + [HBM] * 10,
        out_specs=(VMEM, VMEM, VMEM),
        scratch_shapes=[
            pltpu.SMEM((rows,), jnp.int32),
            pltpu.SMEM((rows,), jnp.int32),
            pltpu.VMEM((1, head), jnp.float32),
            pltpu.VMEM(queries.shape, jnp.bfloat16),
            pltpu.VMEM(new_keys.shape, jnp.bfloat16),
            pltpu.VMEM(new_values.shape, jnp.bfloat16),
            pltpu.VMEM((rows, length, head), jnp.bfloat16),
            pltpu.VMEM((rows, length, head), jnp.bfloat16),
            pltpu.VMEM((cores * chips, depth, share), jnp.bfloat16),
        ]
        + [pltpu.VMEM((pairs, head), jnp.float32)] * 6
        + [
            pltpu.VMEM((flat, head), jnp.float32),
            pltpu.VMEM((pairs, head), jnp.float32),
            pltpu.SemaphoreType.DMA((6,)),
            pltpu.SemaphoreType.DMA((steps,)),
            pltpu.SemaphoreType.DMA((2,)),
            pltpu.SemaphoreType.DMA((cores * chips,)),
        ],
        compiler_params=pltpu.CompilerParams(vmem_limit_bytes=40960 * KIB),
        name="attend",
    )(
        core,
        chip,
        *(
            pltpu.with_memory_space_constraint(array, pltpu.HBM)
            for array in (
                cache_lengths,
                positions,
                jnp.asarray(rates),
                queries,
                new_keys,
                new_values,
                cache_keys,
                cache_values,
                out_weight,
                hidden_in,
            )
        ),
    )

    got = lax.ppermute(send, "core", SWAP)
    paired = lambda part: keep[part] + widen(got[part])
    up = shift(narrow(paired(TO_UP)), 1)
    down = shift(narrow(paired(TO_DOWN)), -1)
    stay = paired(STAY)
    above = shift(narrow(stay[2] + widen(up[2]) + widen(down[1])), 3)
    below = shift(narrow(stay[0] + widen(up[0])), -3)
    update = narrow(stay[1] + widen(up[1]) + widen(down[0]) + widen(above) + widen(below))
    updates = [
        lax.ppermute(update, "section", [(i, i + by) for i in range(sections - by)])
        for by in (1,2,3)
    ]
    updates = [updates[(1,2,3).index(by)] for by in range(sections - 1, 0, -1)] + [update]
    for term in updates:
        current = narrow(widen(current) + widen(term))
    mine = current[None]
    near = [shift(mine, -3), mine, shift(mine, 3)]
    up = shift(jnp.concatenate(near), 1)
    down = shift(jnp.concatenate(near[1:]), -1)
    pieces = near + [up, down]
    pieces = pieces + [
        lax.ppermute(piece, "core", SWAP)
        for piece in (jnp.concatenate(near), up, down)
    ]
    states = pl.pallas_call(
        assemble,
        out_shape=jax.ShapeDtypeStruct((flat, model), jnp.bfloat16),
        in_specs=[SMEM, SMEM] + [ANY] * len(pieces),
        out_specs=HBM,
        scratch_shapes=[pltpu.SemaphoreType.DMA((cores * chips,))],
        compiler_params=pltpu.CompilerParams(vmem_limit_bytes=1024 * KIB),
        name="assemble",
    )(core, chip, *pieces)
    return states.reshape(1, steps, rows, model)


def solution(mesh):
    sizes = dict(mesh.shape)
    split = Mesh(
        mesh.devices.reshape(sizes["dp"], sizes["section"], sizes["tensor"] // 2, 2),
        ("dp", "section", "z", "core"),
    )
    tensor = ("z", "core")
    placed = (
        P(None, "dp", None),
        P("section", None, "dp", tensor),
        P("section", None, "dp", tensor),
        P("section", None, "dp", tensor),
        P("section", "dp", None, tensor),
        P("section", "dp", None, tensor),
        P("section", tensor, None),
        P("dp"),
        P("dp"),
    )
    return jax.shard_map(
        per_device,
        mesh=split,
        in_specs=placed,
        out_specs=P("section", None, "dp", None),
        check_vma=False,
    )
```

```python
import jax
import jax.numpy as jnp
import numpy as np
from jax import lax
from jax.experimental import pallas as pl
from jax.experimental.pallas import tpu as pltpu
from jax.sharding import Mesh
from jax.sharding import PartitionSpec as P

KIB = 1024
OFFSETS = (-2, 1, 4, -1, 2, -3, 0, 3)
TO_UP, TO_DOWN, STAY = slice(0, 3), slice(3, 5), slice(5, 8)
GROUP = 4


def attend(
    core_ref,
    chip_ref,
    length_hbm,
    position_hbm,
    rate_hbm,
    query_hbm,
    new_key_hbm,
    new_value_hbm,
    key_hbm,
    value_hbm,
    weight_hbm,
    hidden_hbm,
    send_ref,
    keep_ref,
    near_ref,
    length_ref,
    position_ref,
    rate_ref,
    query_ref,
    new_key_ref,
    new_value_ref,
    key_ref,
    value_ref,
    weight_ref,
    rotated,
    fresh0,
    fresh1,
    value0,
    value1,
    lengths,
    turns,
    attended,
    small_sem,
    hidden_sem,
    cache_sem,
    weight_sem,
):
    rows, length, head = key_ref.shape
    flat, width = near_ref.shape
    steps = flat // rows
    depth = weight_ref.shape[1]
    group = depth // head
    per_row = steps * group
    chips = send_ref.shape[0]
    factor = head**-0.5
    core = core_ref[0]
    chip = chip_ref[0]

    def columns(half, offset):
        block = half * chips + lax.rem(chip + ((1 - 2 * half) * offset + chips), chips)
        return pl.ds(pl.multiple_of(block * width, width), width)

    small = [
        pltpu.make_async_copy(source, target, small_sem.at[i])
        for i, (source, target) in enumerate(
            (
                (position_hbm, position_ref),
                (rate_hbm, rate_ref),
                (length_hbm, length_ref),
                (new_key_hbm, new_key_ref),
                (query_hbm, query_ref),
                (new_value_hbm, new_value_ref),
            )
        )
    ]
    caches = [
        pltpu.make_async_copy(key_hbm.at[0], key_ref, cache_sem.at[0]),
        pltpu.make_async_copy(value_hbm.at[0], value_ref, cache_sem.at[1]),
    ]
    weights = []
    for half in (1 - core, core):
        for offset in OFFSETS:
            slot = len(weights)
            weights.append(
                pltpu.make_async_copy(
                    weight_hbm.at[0, :, columns(half, offset)],
                    weight_ref.at[slot],
                    weight_sem.at[slot],
                )
            )
    hidden = [
        pltpu.make_async_copy(
            hidden_hbm.at[s, :, columns(core, 0)],
            near_ref.at[s * rows : (s + 1) * rows],
            hidden_sem.at[s],
        )
        for s in range(steps)
    ]
    for copy in small + caches:
        copy.start()

    for copy in small:
        copy.wait()
    for row in range(rows):
        for s in range(steps):
            at = s * rows + row
            when = (position_ref[row] + s).astype(jnp.float32)
            turns[at : at + 1, :] = jnp.full((1, head), when, jnp.float32)
        limit = length_ref[row].astype(jnp.float32)
        lengths[row * per_row : (row + 1) * per_row, :] = jnp.full((per_row, head), limit, jnp.float32)
    sign = jnp.where(lax.broadcasted_iota(jnp.int32, (1, head), 1) < head // 2, -1.0, 1.0)
    turn = turns[...] * rate_ref[...]
    cosine = jnp.cos(turn)
    sine = jnp.sin(turn) * sign

    def rot(v):
        v = v.astype(jnp.float32).reshape(flat, head)
        out = v * cosine + pltpu.roll(v, head // 2, 1) * sine
        return out.astype(jnp.bfloat16).astype(jnp.float32)

    keys = rot(new_key_ref[0])
    fresh = (fresh0, fresh1)
    fresh_values = (value0, value1)
    for g in range(group):
        q = rot(query_ref[0, :, :, g * head : (g + 1) * head])
        for s in range(steps):
            at = pl.ds(s * group + g, rows, stride=per_row)
            mine = q[s * rows : (s + 1) * rows]
            rotated[at, :] = mine
            for m in range(steps):
                if m <= s:
                    score = jnp.sum(mine * keys[m * rows : (m + 1) * rows], axis=-1, keepdims=True)
                    fresh[m][at, :] = jnp.broadcast_to(score * factor, (rows, head))
                else:
                    fresh[m][at, :] = jnp.full((rows, head), -jnp.inf, jnp.float32)
                fresh_values[m][at, :] = new_value_ref[0, m].astype(jnp.float32)

    q_all = rotated[...].astype(jnp.bfloat16)
    caches[0].wait()
    for copy in weights[:chips]:
        copy.start()
    scores = jnp.concatenate(
        [
            lax.dot_general(
                q_all[row * per_row : (row + 1) * per_row],
                key_ref[row],
                (((1,), (1,)), ((), ())),
                preferred_element_type=jnp.float32,
            )
            for row in range(rows)
        ],
        axis=0,
    )
    lane = lax.broadcasted_iota(jnp.int32, (1, length), 1).astype(jnp.float32)
    limit = jnp.concatenate([lengths[...]] * (length // head), axis=1)
    scores = jnp.where(lane < limit, scores * factor, -jnp.inf)
    new0 = fresh0[...]
    new1 = fresh1[...]
    highest = jnp.maximum(
        jnp.max(scores, axis=-1, keepdims=True), jnp.maximum(new0, new1)[:, 0:1]
    )
    past = jnp.exp(scores - highest)
    new0 = jnp.exp(new0 - highest)
    new1 = jnp.exp(new1 - highest)
    total = jnp.sum(past, axis=-1, keepdims=True) + (new0 + new1)[:, 0:1]
    scale = 1.0 / total
    past = (past * scale).astype(jnp.bfloat16)
    new0 = (new0 * scale).astype(jnp.bfloat16).astype(jnp.float32)
    new1 = (new1 * scale).astype(jnp.bfloat16).astype(jnp.float32)
    caches[1].wait()
    for copy in weights[chips:] + hidden:
        copy.start()
    results = jnp.concatenate(
        [
            jnp.dot(
                past[row * per_row : (row + 1) * per_row],
                value_ref[row],
                preferred_element_type=jnp.float32,
            )
            for row in range(rows)
        ],
        axis=0,
    )
    attended[...] = results + new0 * value0[...] + new1 * value1[...]
    left = jnp.concatenate(
        [
            jnp.concatenate(
                [attended[pl.ds(s * group + g, rows, stride=per_row), :] for g in range(group)],
                axis=1,
            )
            for s in range(steps)
        ],
        axis=0,
    ).astype(jnp.bfloat16)
    for first in range(0, len(weights), GROUP):
        for slot in range(first, first + GROUP):
            weights[slot].wait()
        for slot in range(first, first + GROUP):
            partial = jnp.dot(left, weight_ref[slot], preferred_element_type=jnp.float32)
            target = send_ref if slot < chips else keep_ref
            target[slot % chips] = partial.astype(target.dtype)
    for copy in hidden:
        copy.wait()


PIECES = (
    (False, (-2,)),
    (False, (0,)),
    (False, (2,)),
    (False, (4,)),
    (False, (-3, -1)),
    (False, (3, 1)),
    (True, (-2, 0, 2, 4)),
    (True, (-3, -1)),
    (True, (3, 1)),
)


def assemble(core_ref, chip_ref, *refs):
    parts, out_ref, sem = refs[:-2], refs[-2], refs[-1]
    core, chip = core_ref[0], chip_ref[0]
    model = out_ref.shape[1]
    copies = []
    for ref, (swapped, offsets) in zip(parts, PIECES):
        half = 1 - core if swapped else core
        width = ref.shape[-1]
        chips = model // width // 2
        for i, offset in enumerate(offsets):
            block = half * chips + lax.rem(chip + ((1 - 2 * half) * offset + chips), chips)
            at = pl.ds(pl.multiple_of(block * width, width), width)
            copies.append(
                pltpu.make_async_copy(ref.at[i], out_ref.at[:, at], sem.at[len(copies)])
            )
    for copy in copies:
        copy.start()
    for copy in copies:
        copy.wait()


VMEM = pl.BlockSpec(memory_space=pltpu.VMEM)
SMEM = pl.BlockSpec(memory_space=pltpu.SMEM)
HBM = pl.BlockSpec(memory_space=pltpu.HBM)
ANY = pl.BlockSpec(memory_space=pl.ANY)
SWAP = [(0, 1), (1, 0)]


def widen(array):
    return array.astype(jnp.float32)


def narrow(array):
    return array.astype(jnp.bfloat16)


def per_device(
    hidden_in,
    queries,
    new_keys,
    new_values,
    cache_keys,
    cache_values,
    out_weight,
    cache_lengths,
    positions,
):
    cores = lax.axis_size("core")
    chips = lax.axis_size("z")
    sections = lax.axis_size("section")
    steps, rows, model = hidden_in.shape
    length, head = cache_keys.shape[2:]
    depth = queries.shape[3]
    share = model // (cores * chips)
    flat = steps * rows
    pairs = flat * depth // head
    half = head // 2
    rates = np.float32(500000.0) ** (-np.arange(half, dtype=np.float32) * np.float32(2.0 / head))
    rates = np.concatenate([rates, rates]).astype(np.float32)[None]
    core = lax.axis_index("core").astype(jnp.int32).reshape(1)
    chip = lax.axis_index("z").astype(jnp.int32).reshape(1)

    def shift(array, by):
        pairs = []
        for i in range(chips):
            for c in range(cores):
                j = (i + (1 - 2 * c) * by) % chips
                pairs.append((i * cores + c, j * cores + c))
        return lax.ppermute(array, ("z", "core"), pairs)

    send, keep, current = pl.pallas_call(
        attend,
        out_shape=(
            jax.ShapeDtypeStruct((chips, flat, share), jnp.bfloat16),
            jax.ShapeDtypeStruct((chips, flat, share), jnp.float32),
            jax.ShapeDtypeStruct((flat, share), jnp.bfloat16),
        ),
        in_specs=[SMEM, SMEM] + [HBM] * 10,
        out_specs=(VMEM, VMEM, VMEM),
        scratch_shapes=[
            pltpu.SMEM((rows,), jnp.int32),
            pltpu.SMEM((rows,), jnp.int32),
            pltpu.VMEM((1, head), jnp.float32),
            pltpu.VMEM(queries.shape, jnp.bfloat16),
            pltpu.VMEM(new_keys.shape, jnp.bfloat16),
            pltpu.VMEM(new_values.shape, jnp.bfloat16),
            pltpu.VMEM((rows, length, head), jnp.bfloat16),
            pltpu.VMEM((rows, length, head), jnp.bfloat16),
            pltpu.VMEM((cores * chips, depth, share), jnp.bfloat16),
        ]
        + [pltpu.VMEM((pairs, head), jnp.float32)] * 6
        + [
            pltpu.VMEM((flat, head), jnp.float32),
            pltpu.VMEM((pairs, head), jnp.float32),
            pltpu.SemaphoreType.DMA((6,)),
            pltpu.SemaphoreType.DMA((steps,)),
            pltpu.SemaphoreType.DMA((2,)),
            pltpu.SemaphoreType.DMA((cores * chips,)),
        ],
        compiler_params=pltpu.CompilerParams(vmem_limit_bytes=40960 * KIB),
        name="attend",
    )(
        core,
        chip,
        *(
            pltpu.with_memory_space_constraint(array, pltpu.HBM)
            for array in (
                cache_lengths,
                positions,
                jnp.asarray(rates),
                queries,
                new_keys,
                new_values,
                cache_keys,
                cache_values,
                out_weight,
                hidden_in,
            )
        ),
    )

    got = lax.ppermute(send, "core", SWAP)
    paired = lambda part: keep[part] + widen(got[part])
    up = shift(narrow(paired(TO_UP)), 1)
    down = shift(narrow(paired(TO_DOWN)), -1)
    stay = paired(STAY)
    above = shift(narrow(stay[2] + widen(up[2]) + widen(down[1])), 3)
    below = shift(narrow(stay[0] + widen(up[0])), -3)
    update = narrow(stay[1] + widen(up[1]) + widen(down[0]) + widen(above) + widen(below))
    section = lax.axis_index("section")
    updates = [
        jnp.where(
            section >= by,
            lax.ppermute(update, "section", [(i, (i + by) % sections) for i in range(sections)]),
            0,
        )
        for by in (1,2,3)
    ]
    updates = [updates[(1,2,3).index(by)] for by in range(sections - 1, 0, -1)] + [update]
    for term in updates:
        current = narrow(widen(current) + widen(term))
    mine = current[None]
    below = shift(mine, 2)
    above = shift(mine, -2)
    across = shift(mine, 4)
    up = shift(jnp.concatenate([below, mine]), 1)
    down = shift(jnp.concatenate([above, mine]), -1)
    pieces = [below, mine, above, across, up, down]
    pieces += [
        lax.ppermute(piece, "core", SWAP)
        for piece in (jnp.concatenate([below, mine, above, across]), up, down)
    ]
    states = pl.pallas_call(
        assemble,
        out_shape=jax.ShapeDtypeStruct((flat, model), jnp.bfloat16),
        in_specs=[SMEM, SMEM] + [ANY] * len(pieces),
        out_specs=HBM,
        scratch_shapes=[pltpu.SemaphoreType.DMA((cores * chips,))],
        compiler_params=pltpu.CompilerParams(vmem_limit_bytes=1024 * KIB),
        name="assemble",
    )(core, chip, *pieces)
    return states.reshape(1, steps, rows, model)


def solution(mesh):
    sizes = dict(mesh.shape)
    split = Mesh(
        mesh.devices.reshape(sizes["dp"], sizes["section"], sizes["tensor"] // 2, 2),
        ("dp", "section", "z", "core"),
    )
    tensor = ("z", "core")
    placed = (
        P(None, "dp", None),
        P("section", None, "dp", tensor),
        P("section", None, "dp", tensor),
        P("section", None, "dp", tensor),
        P("section", "dp", None, tensor),
        P("section", "dp", None, tensor),
        P("section", tensor, None),
        P("dp"),
        P("dp"),
    )
    return jax.shard_map(
        per_device,
        mesh=split,
        in_specs=placed,
        out_specs=P("section", None, "dp", None),
        check_vma=False,
    )
```

```python
import jax
import jax.numpy as jnp
import numpy as np
from jax import lax
from jax.experimental import pallas as pl
from jax.experimental.pallas import tpu as pltpu
from jax.sharding import Mesh
from jax.sharding import PartitionSpec as P

KIB = 1024
OFFSETS = (1, 3, -1, -3, 4, 2, 0, -2)
TO_UP, TO_DOWN, ACROSS, STAY = slice(0, 2), slice(2, 4), slice(4, 5), slice(5, 8)
GROUP = 4


def attend(
    core_ref,
    chip_ref,
    length_hbm,
    position_hbm,
    rate_hbm,
    query_hbm,
    new_key_hbm,
    new_value_hbm,
    key_hbm,
    value_hbm,
    weight_hbm,
    hidden_hbm,
    send_ref,
    keep_ref,
    near_ref,
    length_ref,
    position_ref,
    rate_ref,
    query_ref,
    new_key_ref,
    new_value_ref,
    key_ref,
    value_ref,
    weight_ref,
    rotated,
    fresh0,
    fresh1,
    value0,
    value1,
    lengths,
    turns,
    attended,
    small_sem,
    hidden_sem,
    cache_sem,
    weight_sem,
):
    rows, length, head = key_ref.shape
    flat, width = near_ref.shape
    steps = flat // rows
    depth = weight_ref.shape[1]
    group = depth // head
    per_row = steps * group
    chips = send_ref.shape[0]
    factor = head**-0.5
    core = core_ref[0]
    chip = chip_ref[0]

    def columns(half, offset):
        block = half * chips + lax.rem(chip + ((1 - 2 * half) * offset + chips), chips)
        return pl.ds(pl.multiple_of(block * width, width), width)

    small = [
        pltpu.make_async_copy(source, target, small_sem.at[i])
        for i, (source, target) in enumerate(
            (
                (position_hbm, position_ref),
                (rate_hbm, rate_ref),
                (length_hbm, length_ref),
                (new_key_hbm, new_key_ref),
                (query_hbm, query_ref),
                (new_value_hbm, new_value_ref),
            )
        )
    ]
    caches = [
        pltpu.make_async_copy(key_hbm.at[0], key_ref, cache_sem.at[0]),
        pltpu.make_async_copy(value_hbm.at[0], value_ref, cache_sem.at[1]),
    ]
    weights = []
    for half in (1 - core, core):
        for offset in OFFSETS:
            slot = len(weights)
            weights.append(
                pltpu.make_async_copy(
                    weight_hbm.at[0, :, columns(half, offset)],
                    weight_ref.at[slot],
                    weight_sem.at[slot],
                )
            )
    hidden = [
        pltpu.make_async_copy(
            hidden_hbm.at[s, :, columns(core, 0)],
            near_ref.at[s * rows : (s + 1) * rows],
            hidden_sem.at[s],
        )
        for s in range(steps)
    ]
    for copy in small + caches:
        copy.start()

    for copy in small:
        copy.wait()
    for row in range(rows):
        for s in range(steps):
            at = s * rows + row
            when = (position_ref[row] + s).astype(jnp.float32)
            turns[at : at + 1, :] = jnp.full((1, head), when, jnp.float32)
        limit = length_ref[row].astype(jnp.float32)
        lengths[row * per_row : (row + 1) * per_row, :] = jnp.full((per_row, head), limit, jnp.float32)
    sign = jnp.where(lax.broadcasted_iota(jnp.int32, (1, head), 1) < head // 2, -1.0, 1.0)
    turn = turns[...] * rate_ref[...]
    cosine = jnp.cos(turn)
    sine = jnp.sin(turn) * sign

    def rot(v):
        v = v.astype(jnp.float32).reshape(flat, head)
        out = v * cosine + pltpu.roll(v, head // 2, 1) * sine
        return out.astype(jnp.bfloat16).astype(jnp.float32)

    keys = rot(new_key_ref[0])
    fresh = (fresh0, fresh1)
    fresh_values = (value0, value1)
    for g in range(group):
        q = rot(query_ref[0, :, :, g * head : (g + 1) * head])
        for s in range(steps):
            at = pl.ds(s * group + g, rows, stride=per_row)
            mine = q[s * rows : (s + 1) * rows]
            rotated[at, :] = mine
            for m in range(steps):
                if m <= s:
                    score = jnp.sum(mine * keys[m * rows : (m + 1) * rows], axis=-1, keepdims=True)
                    fresh[m][at, :] = jnp.broadcast_to(score * factor, (rows, head))
                else:
                    fresh[m][at, :] = jnp.full((rows, head), -jnp.inf, jnp.float32)
                fresh_values[m][at, :] = new_value_ref[0, m].astype(jnp.float32)

    q_all = rotated[...].astype(jnp.bfloat16)
    caches[0].wait()
    for copy in weights[:chips]:
        copy.start()
    scores = jnp.concatenate(
        [
            lax.dot_general(
                q_all[row * per_row : (row + 1) * per_row],
                key_ref[row],
                (((1,), (1,)), ((), ())),
                preferred_element_type=jnp.float32,
            )
            for row in range(rows)
        ],
        axis=0,
    )
    lane = lax.broadcasted_iota(jnp.int32, (1, length), 1).astype(jnp.float32)
    limit = jnp.concatenate([lengths[...]] * (length // head), axis=1)
    scores = jnp.where(lane < limit, scores * factor, -jnp.inf)
    new0 = fresh0[...]
    new1 = fresh1[...]
    highest = jnp.maximum(
        jnp.max(scores, axis=-1, keepdims=True), jnp.maximum(new0, new1)[:, 0:1]
    )
    past = jnp.exp(scores - highest)
    new0 = jnp.exp(new0 - highest)
    new1 = jnp.exp(new1 - highest)
    total = jnp.sum(past, axis=-1, keepdims=True) + (new0 + new1)[:, 0:1]
    scale = 1.0 / total
    past = (past * scale).astype(jnp.bfloat16)
    new0 = (new0 * scale).astype(jnp.bfloat16).astype(jnp.float32)
    new1 = (new1 * scale).astype(jnp.bfloat16).astype(jnp.float32)
    caches[1].wait()
    for copy in weights[chips:] + hidden:
        copy.start()
    results = jnp.concatenate(
        [
            jnp.dot(
                past[row * per_row : (row + 1) * per_row],
                value_ref[row],
                preferred_element_type=jnp.float32,
            )
            for row in range(rows)
        ],
        axis=0,
    )
    attended[...] = results + new0 * value0[...] + new1 * value1[...]
    left = jnp.concatenate(
        [
            jnp.concatenate(
                [attended[pl.ds(s * group + g, rows, stride=per_row), :] for g in range(group)],
                axis=1,
            )
            for s in range(steps)
        ],
        axis=0,
    ).astype(jnp.bfloat16)
    for first in range(0, len(weights), GROUP):
        for slot in range(first, first + GROUP):
            weights[slot].wait()
        for slot in range(first, first + GROUP):
            partial = jnp.dot(left, weight_ref[slot], preferred_element_type=jnp.float32)
            target = send_ref if slot < chips else keep_ref
            target[slot % chips] = partial.astype(target.dtype)
    for copy in hidden:
        copy.wait()


PIECES = (
    (False, (-2,)),
    (False, (0,)),
    (False, (2,)),
    (False, (4,)),
    (False, (-3, -1)),
    (False, (3, 1)),
    (True, (-2, 0, 2, 4)),
    (True, (-3, -1)),
    (True, (3, 1)),
)


def assemble(core_ref, chip_ref, *refs):
    parts, out_ref, sem = refs[:-2], refs[-2], refs[-1]
    core, chip = core_ref[0], chip_ref[0]
    model = out_ref.shape[1]
    copies = []
    for ref, (swapped, offsets) in zip(parts, PIECES):
        half = 1 - core if swapped else core
        width = ref.shape[-1]
        chips = model // width // 2
        for i, offset in enumerate(offsets):
            block = half * chips + lax.rem(chip + ((1 - 2 * half) * offset + chips), chips)
            at = pl.ds(pl.multiple_of(block * width, width), width)
            copies.append(
                pltpu.make_async_copy(ref.at[i], out_ref.at[:, at], sem.at[len(copies)])
            )
    for copy in copies:
        copy.start()
    for copy in copies:
        copy.wait()


VMEM = pl.BlockSpec(memory_space=pltpu.VMEM)
SMEM = pl.BlockSpec(memory_space=pltpu.SMEM)
HBM = pl.BlockSpec(memory_space=pltpu.HBM)
ANY = pl.BlockSpec(memory_space=pl.ANY)
SWAP = [(0, 1), (1, 0)]


def widen(array):
    return array.astype(jnp.float32)


def narrow(array):
    return array.astype(jnp.bfloat16)


def per_device(
    hidden_in,
    queries,
    new_keys,
    new_values,
    cache_keys,
    cache_values,
    out_weight,
    cache_lengths,
    positions,
):
    cores = lax.axis_size("core")
    chips = lax.axis_size("z")
    sections = lax.axis_size("section")
    steps, rows, model = hidden_in.shape
    length, head = cache_keys.shape[2:]
    depth = queries.shape[3]
    share = model // (cores * chips)
    flat = steps * rows
    pairs = flat * depth // head
    half = head // 2
    rates = np.float32(500000.0) ** (-np.arange(half, dtype=np.float32) * np.float32(2.0 / head))
    rates = np.concatenate([rates, rates]).astype(np.float32)[None]
    core = lax.axis_index("core").astype(jnp.int32).reshape(1)
    chip = lax.axis_index("z").astype(jnp.int32).reshape(1)

    def shift(array, by):
        pairs = []
        for i in range(chips):
            for c in range(cores):
                j = (i + (1 - 2 * c) * by) % chips
                pairs.append((i * cores + c, j * cores + c))
        return lax.ppermute(array, ("z", "core"), pairs)

    send, keep, current = pl.pallas_call(
        attend,
        out_shape=(
            jax.ShapeDtypeStruct((chips, flat, share), jnp.bfloat16),
            jax.ShapeDtypeStruct((chips, flat, share), jnp.float32),
            jax.ShapeDtypeStruct((flat, share), jnp.bfloat16),
        ),
        in_specs=[SMEM, SMEM] + [HBM] * 10,
        out_specs=(VMEM, VMEM, VMEM),
        scratch_shapes=[
            pltpu.SMEM((rows,), jnp.int32),
            pltpu.SMEM((rows,), jnp.int32),
            pltpu.VMEM((1, head), jnp.float32),
            pltpu.VMEM(queries.shape, jnp.bfloat16),
            pltpu.VMEM(new_keys.shape, jnp.bfloat16),
            pltpu.VMEM(new_values.shape, jnp.bfloat16),
            pltpu.VMEM((rows, length, head), jnp.bfloat16),
            pltpu.VMEM((rows, length, head), jnp.bfloat16),
            pltpu.VMEM((cores * chips, depth, share), jnp.bfloat16),
        ]
        + [pltpu.VMEM((pairs, head), jnp.float32)] * 6
        + [
            pltpu.VMEM((flat, head), jnp.float32),
            pltpu.VMEM((pairs, head), jnp.float32),
            pltpu.SemaphoreType.DMA((6,)),
            pltpu.SemaphoreType.DMA((steps,)),
            pltpu.SemaphoreType.DMA((2,)),
            pltpu.SemaphoreType.DMA((cores * chips,)),
        ],
        compiler_params=pltpu.CompilerParams(vmem_limit_bytes=40960 * KIB),
        name="attend",
    )(
        core,
        chip,
        *(
            pltpu.with_memory_space_constraint(array, pltpu.HBM)
            for array in (
                cache_lengths,
                positions,
                jnp.asarray(rates),
                queries,
                new_keys,
                new_values,
                cache_keys,
                cache_values,
                out_weight,
                hidden_in,
            )
        ),
    )

    got = lax.ppermute(send, "core", SWAP)
    paired = lambda part: keep[part] + widen(got[part])
    up, down, across, stay = lax.optimization_barrier(
        (narrow(paired(TO_UP)), narrow(paired(TO_DOWN)), narrow(paired(ACROSS)), paired(STAY))
    )
    up = shift(up, 1)
    down = shift(down, -1)
    across = shift(across, 4)
    above = shift(narrow(stay[0] + widen(up[1])), 2)
    below = shift(narrow(stay[2] + widen(down[1])), -2)
    update = stay[1] + widen(up[0]) + widen(down[0]) + widen(across[0])
    update = narrow(update + widen(above) + widen(below))
    section = lax.axis_index("section")
    updates = [
        jnp.where(
            section >= by,
            lax.ppermute(update, "section", [(i, (i + by) % sections) for i in range(sections)]),
            0,
        )
        for by in (1,2,3)
    ]
    updates = [updates[(1,2,3).index(by)] for by in range(sections - 1, 0, -1)] + [update]
    for term in updates:
        current = narrow(widen(current) + widen(term))
    mine = current[None]
    below = shift(mine, 2)
    above = shift(mine, -2)
    across = shift(mine, 4)
    up = shift(jnp.concatenate([below, mine]), 1)
    down = shift(jnp.concatenate([above, mine]), -1)
    pieces = [below, mine, above, across, up, down]
    pieces += [
        lax.ppermute(piece, "core", SWAP)
        for piece in (jnp.concatenate([below, mine, above, across]), up, down)
    ]
    states = pl.pallas_call(
        assemble,
        out_shape=jax.ShapeDtypeStruct((flat, model), jnp.bfloat16),
        in_specs=[SMEM, SMEM] + [ANY] * len(pieces),
        out_specs=HBM,
        scratch_shapes=[pltpu.SemaphoreType.DMA((cores * chips,))],
        compiler_params=pltpu.CompilerParams(vmem_limit_bytes=1024 * KIB),
        name="assemble",
    )(core, chip, *pieces)
    return states.reshape(1, steps, rows, model)


def solution(mesh):
    sizes = dict(mesh.shape)
    split = Mesh(
        mesh.devices.reshape(sizes["dp"], sizes["section"], sizes["tensor"] // 2, 2),
        ("dp", "section", "z", "core"),
    )
    tensor = ("z", "core")
    placed = (
        P(None, "dp", None),
        P("section", None, "dp", tensor),
        P("section", None, "dp", tensor),
        P("section", None, "dp", tensor),
        P("section", "dp", None, tensor),
        P("section", "dp", None, tensor),
        P("section", tensor, None),
        P("dp"),
        P("dp"),
    )
    return jax.shard_map(
        per_device,
        mesh=split,
        in_specs=placed,
        out_specs=P("section", None, "dp", None),
        check_vma=False,
    )
```

```python
import jax
import jax.numpy as jnp
import numpy as np
from jax import lax
from jax.experimental import pallas as pl
from jax.experimental.pallas import tpu as pltpu
from jax.sharding import Mesh
from jax.sharding import PartitionSpec as P

KIB = 1024
OFFSETS = (1, 3, -1, -3, 4, 2, 0, -2)
TO_UP, TO_DOWN, ACROSS, STAY = slice(0, 2), slice(2, 4), slice(4, 5), slice(5, 8)
EARLY = 4
GROUP = 4


def attend(
    core_ref,
    chip_ref,
    length_hbm,
    position_hbm,
    rate_hbm,
    query_hbm,
    new_key_hbm,
    new_value_hbm,
    key_hbm,
    value_hbm,
    weight_hbm,
    hidden_hbm,
    first_ref,
    second_ref,
    keep_ref,
    near_ref,
    length_ref,
    position_ref,
    rate_ref,
    query_ref,
    new_key_ref,
    new_value_ref,
    key_ref,
    value_ref,
    weight_ref,
    rotated,
    fresh0,
    fresh1,
    value0,
    value1,
    lengths,
    turns,
    attended,
    small_sem,
    hidden_sem,
    cache_sem,
    weight_sem,
):
    rows, length, head = key_ref.shape
    flat, width = near_ref.shape
    steps = flat // rows
    depth = weight_ref.shape[1]
    group = depth // head
    per_row = steps * group
    chips = keep_ref.shape[0]
    early = first_ref.shape[0]
    factor = head**-0.5
    core = core_ref[0]
    chip = chip_ref[0]

    def columns(half, offset):
        block = half * chips + lax.rem(chip + ((1 - 2 * half) * offset + chips), chips)
        return pl.ds(pl.multiple_of(block * width, width), width)

    small = [
        pltpu.make_async_copy(source, target, small_sem.at[i])
        for i, (source, target) in enumerate(
            (
                (position_hbm, position_ref),
                (rate_hbm, rate_ref),
                (length_hbm, length_ref),
                (new_key_hbm, new_key_ref),
                (query_hbm, query_ref),
                (new_value_hbm, new_value_ref),
            )
        )
    ]
    caches = [
        pltpu.make_async_copy(key_hbm.at[0], key_ref, cache_sem.at[0]),
        pltpu.make_async_copy(value_hbm.at[0], value_ref, cache_sem.at[1]),
    ]
    weights = []
    for half in (1 - core, core):
        for offset in OFFSETS:
            slot = len(weights)
            weights.append(
                pltpu.make_async_copy(
                    weight_hbm.at[0, :, columns(half, offset)],
                    weight_ref.at[slot],
                    weight_sem.at[slot],
                )
            )
    hidden = [
        pltpu.make_async_copy(
            hidden_hbm.at[s, :, columns(core, 0)],
            near_ref.at[s * rows : (s + 1) * rows],
            hidden_sem.at[s],
        )
        for s in range(steps)
    ]
    for copy in small + caches:
        copy.start()

    for copy in small:
        copy.wait()
    for row in range(rows):
        for s in range(steps):
            at = s * rows + row
            when = (position_ref[row] + s).astype(jnp.float32)
            turns[at : at + 1, :] = jnp.full((1, head), when, jnp.float32)
        limit = length_ref[row].astype(jnp.float32)
        lengths[row * per_row : (row + 1) * per_row, :] = jnp.full((per_row, head), limit, jnp.float32)
    sign = jnp.where(lax.broadcasted_iota(jnp.int32, (1, head), 1) < head // 2, -1.0, 1.0)
    turn = turns[...] * rate_ref[...]
    cosine = jnp.cos(turn)
    sine = jnp.sin(turn) * sign

    def rot(v):
        v = v.astype(jnp.float32).reshape(flat, head)
        out = v * cosine + pltpu.roll(v, head // 2, 1) * sine
        return out.astype(jnp.bfloat16).astype(jnp.float32)

    keys = rot(new_key_ref[0])
    fresh = (fresh0, fresh1)
    fresh_values = (value0, value1)
    for g in range(group):
        q = rot(query_ref[0, :, :, g * head : (g + 1) * head])
        for s in range(steps):
            at = pl.ds(s * group + g, rows, stride=per_row)
            mine = q[s * rows : (s + 1) * rows]
            rotated[at, :] = mine
            for m in range(steps):
                if m <= s:
                    score = jnp.sum(mine * keys[m * rows : (m + 1) * rows], axis=-1, keepdims=True)
                    fresh[m][at, :] = jnp.broadcast_to(score * factor, (rows, head))
                else:
                    fresh[m][at, :] = jnp.full((rows, head), -jnp.inf, jnp.float32)
                fresh_values[m][at, :] = new_value_ref[0, m].astype(jnp.float32)

    q_all = rotated[...].astype(jnp.bfloat16)
    caches[0].wait()
    for copy in weights[:chips]:
        copy.start()
    scores = jnp.concatenate(
        [
            lax.dot_general(
                q_all[row * per_row : (row + 1) * per_row],
                key_ref[row],
                (((1,), (1,)), ((), ())),
                preferred_element_type=jnp.float32,
            )
            for row in range(rows)
        ],
        axis=0,
    )
    lane = lax.broadcasted_iota(jnp.int32, (1, length), 1).astype(jnp.float32)
    limit = jnp.concatenate([lengths[...]] * (length // head), axis=1)
    scores = jnp.where(lane < limit, scores * factor, -jnp.inf)
    new0 = fresh0[...]
    new1 = fresh1[...]
    highest = jnp.maximum(
        jnp.max(scores, axis=-1, keepdims=True), jnp.maximum(new0, new1)[:, 0:1]
    )
    past = jnp.exp(scores - highest)
    new0 = jnp.exp(new0 - highest)
    new1 = jnp.exp(new1 - highest)
    total = jnp.sum(past, axis=-1, keepdims=True) + (new0 + new1)[:, 0:1]
    scale = 1.0 / total
    past = (past * scale).astype(jnp.bfloat16)
    new0 = (new0 * scale).astype(jnp.bfloat16).astype(jnp.float32)
    new1 = (new1 * scale).astype(jnp.bfloat16).astype(jnp.float32)
    caches[1].wait()
    for copy in weights[chips:] + hidden:
        copy.start()
    results = jnp.concatenate(
        [
            jnp.dot(
                past[row * per_row : (row + 1) * per_row],
                value_ref[row],
                preferred_element_type=jnp.float32,
            )
            for row in range(rows)
        ],
        axis=0,
    )
    attended[...] = results + new0 * value0[...] + new1 * value1[...]
    left = jnp.concatenate(
        [
            jnp.concatenate(
                [attended[pl.ds(s * group + g, rows, stride=per_row), :] for g in range(group)],
                axis=1,
            )
            for s in range(steps)
        ],
        axis=0,
    ).astype(jnp.bfloat16)
    for first in range(0, len(weights), GROUP):
        for slot in range(first, first + GROUP):
            weights[slot].wait()
        for slot in range(first, first + GROUP):
            partial = jnp.dot(left, weight_ref[slot], preferred_element_type=jnp.float32)
            if slot < early:
                first_ref[slot] = partial.astype(first_ref.dtype)
            elif slot < chips:
                second_ref[slot - early] = partial.astype(second_ref.dtype)
            else:
                keep_ref[slot - chips] = partial
    for copy in hidden:
        copy.wait()


PIECES = (
    (False, (-2,)),
    (False, (0,)),
    (False, (2,)),
    (False, (4,)),
    (False, (-3, -1)),
    (False, (3, 1)),
    (True, (0,)),
    (True, (-2, 2, 4)),
    (True, (-3, -1)),
    (True, (3, 1)),
)


def assemble(core_ref, chip_ref, *refs):
    parts, out_ref, sem = refs[:-2], refs[-2], refs[-1]
    core, chip = core_ref[0], chip_ref[0]
    model = out_ref.shape[1]
    copies = []
    for ref, (swapped, offsets) in zip(parts, PIECES):
        half = 1 - core if swapped else core
        width = ref.shape[-1]
        chips = model // width // 2
        for i, offset in enumerate(offsets):
            block = half * chips + lax.rem(chip + ((1 - 2 * half) * offset + chips), chips)
            at = pl.ds(pl.multiple_of(block * width, width), width)
            copies.append(
                pltpu.make_async_copy(ref.at[i], out_ref.at[:, at], sem.at[len(copies)])
            )
    for copy in copies:
        copy.start()
    for copy in copies:
        copy.wait()


VMEM = pl.BlockSpec(memory_space=pltpu.VMEM)
SMEM = pl.BlockSpec(memory_space=pltpu.SMEM)
HBM = pl.BlockSpec(memory_space=pltpu.HBM)
ANY = pl.BlockSpec(memory_space=pl.ANY)
SWAP = [(0, 1), (1, 0)]


def widen(array):
    return array.astype(jnp.float32)


def narrow(array):
    return array.astype(jnp.bfloat16)


def per_device(
    hidden_in,
    queries,
    new_keys,
    new_values,
    cache_keys,
    cache_values,
    out_weight,
    cache_lengths,
    positions,
):
    cores = lax.axis_size("core")
    chips = lax.axis_size("z")
    sections = lax.axis_size("section")
    steps, rows, model = hidden_in.shape
    length, head = cache_keys.shape[2:]
    depth = queries.shape[3]
    share = model // (cores * chips)
    flat = steps * rows
    pairs = flat * depth // head
    half = head // 2
    rates = np.float32(500000.0) ** (-np.arange(half, dtype=np.float32) * np.float32(2.0 / head))
    rates = np.concatenate([rates, rates]).astype(np.float32)[None]
    core = lax.axis_index("core").astype(jnp.int32).reshape(1)
    chip = lax.axis_index("z").astype(jnp.int32).reshape(1)

    def shift(array, by):
        pairs = []
        for i in range(chips):
            for c in range(cores):
                j = (i + (1 - 2 * c) * by) % chips
                pairs.append((i * cores + c, j * cores + c))
        return lax.ppermute(array, ("z", "core"), pairs)

    first, second, keep, current = pl.pallas_call(
        attend,
        out_shape=(
            jax.ShapeDtypeStruct((EARLY, flat, share), jnp.bfloat16),
            jax.ShapeDtypeStruct((chips - EARLY, flat, share), jnp.bfloat16),
            jax.ShapeDtypeStruct((chips, flat, share), jnp.float32),
            jax.ShapeDtypeStruct((flat, share), jnp.bfloat16),
        ),
        in_specs=[SMEM, SMEM] + [HBM] * 10,
        out_specs=(VMEM, VMEM, VMEM, VMEM),
        scratch_shapes=[
            pltpu.SMEM((rows,), jnp.int32),
            pltpu.SMEM((rows,), jnp.int32),
            pltpu.VMEM((1, head), jnp.float32),
            pltpu.VMEM(queries.shape, jnp.bfloat16),
            pltpu.VMEM(new_keys.shape, jnp.bfloat16),
            pltpu.VMEM(new_values.shape, jnp.bfloat16),
            pltpu.VMEM((rows, length, head), jnp.bfloat16),
            pltpu.VMEM((rows, length, head), jnp.bfloat16),
            pltpu.VMEM((cores * chips, depth, share), jnp.bfloat16),
        ]
        + [pltpu.VMEM((pairs, head), jnp.float32)] * 6
        + [
            pltpu.VMEM((flat, head), jnp.float32),
            pltpu.VMEM((pairs, head), jnp.float32),
            pltpu.SemaphoreType.DMA((6,)),
            pltpu.SemaphoreType.DMA((steps,)),
            pltpu.SemaphoreType.DMA((2,)),
            pltpu.SemaphoreType.DMA((cores * chips,)),
        ],
        compiler_params=pltpu.CompilerParams(vmem_limit_bytes=40960 * KIB),
        name="attend",
    )(
        core,
        chip,
        *(
            pltpu.with_memory_space_constraint(array, pltpu.HBM)
            for array in (
                cache_lengths,
                positions,
                jnp.asarray(rates),
                queries,
                new_keys,
                new_values,
                cache_keys,
                cache_values,
                out_weight,
                hidden_in,
            )
        ),
    )

    first = lax.ppermute(first, "core", SWAP)
    second = lax.ppermute(second, "core", SWAP)

    def paired(part):
        if part.stop <= EARLY:
            return keep[part] + widen(first[part])
        return keep[part] + widen(second[part.start - EARLY : part.stop - EARLY])

    up, down = lax.optimization_barrier((narrow(paired(TO_UP)), narrow(paired(TO_DOWN))))
    across, stay = lax.optimization_barrier((narrow(paired(ACROSS)), paired(STAY)))
    up = shift(up, 1)
    down = shift(down, -1)
    across = shift(across, 4)
    above = shift(narrow(stay[0] + widen(up[1])), 2)
    below = shift(narrow(stay[2] + widen(down[1])), -2)
    update = stay[1] + widen(up[0]) + widen(down[0]) + widen(across[0])
    update = narrow(update + widen(above) + widen(below))
    section = lax.axis_index("section")
    updates = [
        jnp.where(
            section >= by,
            lax.ppermute(update, "section", [(i, (i + by) % sections) for i in range(sections)]),
            0,
        )
        for by in (1,2,3)
    ]
    updates = [updates[(1,2,3).index(by)] for by in range(sections - 1, 0, -1)] + [update]
    for term in updates:
        current = narrow(widen(current) + widen(term))
    mine = current[None]
    below = shift(mine, 2)
    above = shift(mine, -2)
    across = shift(mine, 4)
    up = shift(jnp.concatenate([below, mine]), 1)
    down = shift(jnp.concatenate([above, mine]), -1)
    pieces = [below, mine, above, across, up, down]
    pieces += [
        lax.ppermute(piece, "core", SWAP)
        for piece in (mine, jnp.concatenate([below, above, across]), up, down)
    ]
    states = pl.pallas_call(
        assemble,
        out_shape=jax.ShapeDtypeStruct((flat, model), jnp.bfloat16),
        in_specs=[SMEM, SMEM] + [ANY] * len(pieces),
        out_specs=HBM,
        scratch_shapes=[pltpu.SemaphoreType.DMA((cores * chips,))],
        compiler_params=pltpu.CompilerParams(vmem_limit_bytes=1024 * KIB),
        name="assemble",
    )(core, chip, *pieces)
    return states.reshape(1, steps, rows, model)


def solution(mesh):
    sizes = dict(mesh.shape)
    split = Mesh(
        mesh.devices.reshape(sizes["dp"], sizes["section"], sizes["tensor"] // 2, 2),
        ("dp", "section", "z", "core"),
    )
    tensor = ("z", "core")
    placed = (
        P(None, "dp", None),
        P("section", None, "dp", tensor),
        P("section", None, "dp", tensor),
        P("section", None, "dp", tensor),
        P("section", "dp", None, tensor),
        P("section", "dp", None, tensor),
        P("section", tensor, None),
        P("dp"),
        P("dp"),
    )
    return jax.shard_map(
        per_device,
        mesh=split,
        in_specs=placed,
        out_specs=P("section", None, "dp", None),
        check_vma=False,
    )
```

```python
import jax
import jax.numpy as jnp
import numpy as np
from jax import lax
from jax.experimental import pallas as pl
from jax.experimental.pallas import tpu as pltpu
from jax.sharding import Mesh
from jax.sharding import PartitionSpec as P

KIB = 1024
OFFSETS = (1, 3, -1, -3, 4, 2, 0, -2)
TO_UP, TO_DOWN, ACROSS, STAY = slice(0, 2), slice(2, 4), slice(4, 5), slice(5, 8)
GROUP = 4


def attend(
    core_ref,
    chip_ref,
    length_hbm,
    position_hbm,
    rate_hbm,
    query_hbm,
    new_key_hbm,
    new_value_hbm,
    key_hbm,
    value_hbm,
    weight_hbm,
    hidden_hbm,
    send_ref,
    keep_ref,
    near_ref,
    length_ref,
    position_ref,
    rate_ref,
    query_ref,
    new_key_ref,
    new_value_ref,
    key_ref,
    value_ref,
    weight_ref,
    rotated,
    fresh0,
    fresh1,
    value0,
    value1,
    lengths,
    turns,
    attended,
    small_sem,
    hidden_sem,
    cache_sem,
    weight_sem,
):
    rows, length, head = key_ref.shape
    flat, width = near_ref.shape
    steps = flat // rows
    depth = weight_ref.shape[1]
    group = depth // head
    per_row = steps * group
    chips = send_ref.shape[0]
    factor = head**-0.5
    core = core_ref[0]
    chip = chip_ref[0]

    def columns(half, offset):
        block = half * chips + lax.rem(chip + ((1 - 2 * half) * offset + chips), chips)
        return pl.ds(pl.multiple_of(block * width, width), width)

    small = [
        pltpu.make_async_copy(source, target, small_sem.at[i])
        for i, (source, target) in enumerate(
            (
                (position_hbm, position_ref),
                (rate_hbm, rate_ref),
                (length_hbm, length_ref),
                (new_key_hbm, new_key_ref),
                (query_hbm, query_ref),
                (new_value_hbm, new_value_ref),
            )
        )
    ]
    caches = [
        pltpu.make_async_copy(key_hbm.at[0], key_ref, cache_sem.at[0]),
        pltpu.make_async_copy(value_hbm.at[0], value_ref, cache_sem.at[1]),
    ]
    weights = []
    for half in (1 - core, core):
        for offset in OFFSETS:
            slot = len(weights)
            weights.append(
                pltpu.make_async_copy(
                    weight_hbm.at[0, :, columns(half, offset)],
                    weight_ref.at[slot],
                    weight_sem.at[slot],
                )
            )
    hidden = [
        pltpu.make_async_copy(
            hidden_hbm.at[s, :, columns(core, 0)],
            near_ref.at[s * rows : (s + 1) * rows],
            hidden_sem.at[s],
        )
        for s in range(steps)
    ]
    for copy in small + caches:
        copy.start()

    for copy in small:
        copy.wait()
    for row in range(rows):
        for s in range(steps):
            at = s * rows + row
            when = (position_ref[row] + s).astype(jnp.float32)
            turns[at : at + 1, :] = jnp.full((1, head), when, jnp.float32)
        limit = length_ref[row].astype(jnp.float32)
        lengths[row * per_row : (row + 1) * per_row, :] = jnp.full((per_row, head), limit, jnp.float32)
    sign = jnp.where(lax.broadcasted_iota(jnp.int32, (1, head), 1) < head // 2, -1.0, 1.0)
    turn = turns[...] * rate_ref[...]
    cosine = jnp.cos(turn)
    sine = jnp.sin(turn) * sign

    def rot(v):
        v = v.astype(jnp.float32).reshape(flat, head)
        out = v * cosine + pltpu.roll(v, head // 2, 1) * sine
        return out.astype(jnp.bfloat16).astype(jnp.float32)

    keys = rot(new_key_ref[0])
    fresh = (fresh0, fresh1)
    fresh_values = (value0, value1)
    for g in range(group):
        q = rot(query_ref[0, :, :, g * head : (g + 1) * head])
        for s in range(steps):
            at = pl.ds(s * group + g, rows, stride=per_row)
            mine = q[s * rows : (s + 1) * rows]
            rotated[at, :] = mine
            for m in range(steps):
                if m <= s:
                    score = jnp.sum(mine * keys[m * rows : (m + 1) * rows], axis=-1, keepdims=True)
                    fresh[m][at, :] = jnp.broadcast_to(score * factor, (rows, head))
                else:
                    fresh[m][at, :] = jnp.full((rows, head), -jnp.inf, jnp.float32)
                fresh_values[m][at, :] = new_value_ref[0, m].astype(jnp.float32)

    q_all = rotated[...].astype(jnp.bfloat16)
    caches[0].wait()
    for copy in weights[:chips]:
        copy.start()
    scores = jnp.concatenate(
        [
            lax.dot_general(
                q_all[row * per_row : (row + 1) * per_row],
                key_ref[row],
                (((1,), (1,)), ((), ())),
                preferred_element_type=jnp.float32,
            )
            for row in range(rows)
        ],
        axis=0,
    )
    lane = lax.broadcasted_iota(jnp.int32, (1, length), 1).astype(jnp.float32)
    limit = jnp.concatenate([lengths[...]] * (length // head), axis=1)
    scores = jnp.where(lane < limit, scores * factor, -jnp.inf)
    new0 = fresh0[...]
    new1 = fresh1[...]
    highest = jnp.maximum(
        jnp.max(scores, axis=-1, keepdims=True), jnp.maximum(new0, new1)[:, 0:1]
    )
    past = jnp.exp(scores - highest)
    new0 = jnp.exp(new0 - highest)
    new1 = jnp.exp(new1 - highest)
    total = jnp.sum(past, axis=-1, keepdims=True) + (new0 + new1)[:, 0:1]
    scale = 1.0 / total
    past = (past * scale).astype(jnp.bfloat16)
    new0 = (new0 * scale).astype(jnp.bfloat16).astype(jnp.float32)
    new1 = (new1 * scale).astype(jnp.bfloat16).astype(jnp.float32)
    caches[1].wait()
    for copy in weights[chips:] + hidden:
        copy.start()
    results = jnp.concatenate(
        [
            jnp.dot(
                past[row * per_row : (row + 1) * per_row],
                value_ref[row],
                preferred_element_type=jnp.float32,
            )
            for row in range(rows)
        ],
        axis=0,
    )
    attended[...] = results + new0 * value0[...] + new1 * value1[...]
    left = jnp.concatenate(
        [
            jnp.concatenate(
                [attended[pl.ds(s * group + g, rows, stride=per_row), :] for g in range(group)],
                axis=1,
            )
            for s in range(steps)
        ],
        axis=0,
    ).astype(jnp.bfloat16)
    for first in range(0, len(weights), GROUP):
        for slot in range(first, first + GROUP):
            weights[slot].wait()
        for slot in range(first, first + GROUP):
            partial = jnp.dot(left, weight_ref[slot], preferred_element_type=jnp.float32)
            target = send_ref if slot < chips else keep_ref
            target[slot % chips] = partial.astype(target.dtype)
    for copy in hidden:
        copy.wait()


PIECES = (
    (False, (-2,)),
    (False, (0,)),
    (False, (2,)),
    (False, (4,)),
    (False, (-3, -1)),
    (False, (3, 1)),
    (True, (-2, 0, 2, 4)),
    (True, (-3, -1, 3, 1)),
)


def assemble(core_ref, chip_ref, *refs):
    parts, out_ref, sem = refs[:-2], refs[-2], refs[-1]
    core, chip = core_ref[0], chip_ref[0]
    model = out_ref.shape[1]
    copies = []
    for ref, (swapped, offsets) in zip(parts, PIECES):
        half = 1 - core if swapped else core
        width = ref.shape[-1]
        chips = model // width // 2
        for i, offset in enumerate(offsets):
            block = half * chips + lax.rem(chip + ((1 - 2 * half) * offset + chips), chips)
            at = pl.ds(pl.multiple_of(block * width, width), width)
            copies.append(
                pltpu.make_async_copy(ref.at[i], out_ref.at[:, at], sem.at[len(copies)])
            )
    for copy in copies:
        copy.start()
    for copy in copies:
        copy.wait()


VMEM = pl.BlockSpec(memory_space=pltpu.VMEM)
SMEM = pl.BlockSpec(memory_space=pltpu.SMEM)
HBM = pl.BlockSpec(memory_space=pltpu.HBM)
ANY = pl.BlockSpec(memory_space=pl.ANY)
SWAP = [(0, 1), (1, 0)]


def widen(array):
    return array.astype(jnp.float32)


def narrow(array):
    return array.astype(jnp.bfloat16)


def per_device(
    hidden_in,
    queries,
    new_keys,
    new_values,
    cache_keys,
    cache_values,
    out_weight,
    cache_lengths,
    positions,
):
    cores = lax.axis_size("core")
    chips = lax.axis_size("z")
    sections = lax.axis_size("section")
    steps, rows, model = hidden_in.shape
    length, head = cache_keys.shape[2:]
    depth = queries.shape[3]
    share = model // (cores * chips)
    flat = steps * rows
    pairs = flat * depth // head
    half = head // 2
    rates = np.float32(500000.0) ** (-np.arange(half, dtype=np.float32) * np.float32(2.0 / head))
    rates = np.concatenate([rates, rates]).astype(np.float32)[None]
    core = lax.axis_index("core").astype(jnp.int32).reshape(1)
    chip = lax.axis_index("z").astype(jnp.int32).reshape(1)

    def shift(array, by):
        pairs = []
        for i in range(chips):
            for c in range(cores):
                j = (i + (1 - 2 * c) * by) % chips
                pairs.append((i * cores + c, j * cores + c))
        return lax.ppermute(array, ("z", "core"), pairs)

    send, keep, current = pl.pallas_call(
        attend,
        out_shape=(
            jax.ShapeDtypeStruct((chips, flat, share), jnp.bfloat16),
            jax.ShapeDtypeStruct((chips, flat, share), jnp.float32),
            jax.ShapeDtypeStruct((flat, share), jnp.bfloat16),
        ),
        in_specs=[SMEM, SMEM] + [HBM] * 10,
        out_specs=(VMEM, VMEM, VMEM),
        scratch_shapes=[
            pltpu.SMEM((rows,), jnp.int32),
            pltpu.SMEM((rows,), jnp.int32),
            pltpu.VMEM((1, head), jnp.float32),
            pltpu.VMEM(queries.shape, jnp.bfloat16),
            pltpu.VMEM(new_keys.shape, jnp.bfloat16),
            pltpu.VMEM(new_values.shape, jnp.bfloat16),
            pltpu.VMEM((rows, length, head), jnp.bfloat16),
            pltpu.VMEM((rows, length, head), jnp.bfloat16),
            pltpu.VMEM((cores * chips, depth, share), jnp.bfloat16),
        ]
        + [pltpu.VMEM((pairs, head), jnp.float32)] * 6
        + [
            pltpu.VMEM((flat, head), jnp.float32),
            pltpu.VMEM((pairs, head), jnp.float32),
            pltpu.SemaphoreType.DMA((6,)),
            pltpu.SemaphoreType.DMA((steps,)),
            pltpu.SemaphoreType.DMA((2,)),
            pltpu.SemaphoreType.DMA((cores * chips,)),
        ],
        compiler_params=pltpu.CompilerParams(vmem_limit_bytes=40960 * KIB),
        name="attend",
    )(
        core,
        chip,
        *(
            pltpu.with_memory_space_constraint(array, pltpu.HBM)
            for array in (
                cache_lengths,
                positions,
                jnp.asarray(rates),
                queries,
                new_keys,
                new_values,
                cache_keys,
                cache_values,
                out_weight,
                hidden_in,
            )
        ),
    )

    got = lax.ppermute(send, "core", SWAP)
    paired = lambda part: keep[part] + widen(got[part])
    up, down, across, stay = lax.optimization_barrier(
        (narrow(paired(TO_UP)), narrow(paired(TO_DOWN)), narrow(paired(ACROSS)), paired(STAY))
    )
    up = shift(up, 1)
    down = shift(down, -1)
    across = shift(across, 4)
    above = shift(narrow(stay[0] + widen(up[1])), 2)
    below = shift(narrow(stay[2] + widen(down[1])), -2)
    update = stay[1] + widen(up[0]) + widen(down[0]) + widen(across[0])
    update = narrow(update + widen(above) + widen(below))
    section = lax.axis_index("section")
    updates = [
        jnp.where(
            section >= by,
            lax.ppermute(update, "section", [(i, (i + by) % sections) for i in range(sections)]),
            0,
        )
        for by in (1,2,3)
    ]
    updates = [updates[(1,2,3).index(by)] for by in range(sections - 1, 0, -1)] + [update]
    for term in updates:
        current = narrow(widen(current) + widen(term))
    mine = current[None]
    below = shift(mine, 2)
    above = shift(mine, -2)
    across = shift(mine, 4)
    up = shift(jnp.concatenate([below, mine]), 1)
    down = shift(jnp.concatenate([above, mine]), -1)
    pieces = [below, mine, above, across, up, down]
    pieces += [
        lax.ppermute(piece, "core", SWAP)
        for piece in (jnp.concatenate([below, mine, above, across]), jnp.concatenate([up, down]))
    ]
    states = pl.pallas_call(
        assemble,
        out_shape=jax.ShapeDtypeStruct((flat, model), jnp.bfloat16),
        in_specs=[SMEM, SMEM] + [ANY] * len(pieces),
        out_specs=HBM,
        scratch_shapes=[pltpu.SemaphoreType.DMA((cores * chips,))],
        compiler_params=pltpu.CompilerParams(vmem_limit_bytes=1024 * KIB),
        name="assemble",
    )(core, chip, *pieces)
    return states.reshape(1, steps, rows, model)


def solution(mesh):
    sizes = dict(mesh.shape)
    split = Mesh(
        mesh.devices.reshape(sizes["dp"], sizes["section"], sizes["tensor"] // 2, 2),
        ("dp", "section", "z", "core"),
    )
    tensor = ("z", "core")
    placed = (
        P(None, "dp", None),
        P("section", None, "dp", tensor),
        P("section", None, "dp", tensor),
        P("section", None, "dp", tensor),
        P("section", "dp", None, tensor),
        P("section", "dp", None, tensor),
        P("section", tensor, None),
        P("dp"),
        P("dp"),
    )
    return jax.shard_map(
        per_device,
        mesh=split,
        in_specs=placed,
        out_specs=P("section", None, "dp", None),
        check_vma=False,
    )
```
